256 devices in a mesh: rep: 2 (over y_lo), wide: 16 (over z, core), narrow: 8 (over y_hi, x).
Axes of the slice: x: 4, y: 4 (y_hi: 2, y_lo: 2; y = y_hi * 2 + y_lo), z: 8, core: 2. Of those that a mesh axis runs over, the one named last changes fastest.
Arguments:
- tokens: bfloat16 [256, 256, 1280], P(('rep', 'wide', 'narrow')), may hold values from -24 to 24
- routing: bfloat16 [1280, 128], replicated, may hold values from -1 to 1
- grad_out: bfloat16 [256, 256, 1280], P(('rep', 'wide', 'narrow')), may hold values from -1.5 to 1.5
- slot_out: bfloat16 [256, 128, 1280], P(('rep', 'wide', 'narrow')), may hold values from -6 to 6
- w_first: bfloat16 [64, 1280, 4096], P(('rep', 'wide'), None, 'narrow'), may hold values from -0.15625 to 0.15625
- w_second: bfloat16 [64, 4096, 1280], P(('rep', 'wide'), 'narrow'), may hold values from -0.09375 to 0.09375
Outputs:
- grad_tokens: bfloat16 [256, 256, 1280], P(('rep', 'wide', 'narrow'))
- grad_routing: float32 [1280, 128], P(('rep', 'wide', 'narrow'))
- grad_first: bfloat16 [64, 1280, 4096], P(('rep', 'wide'), None, 'narrow')
- grad_second: bfloat16 [64, 4096, 1280], P(('rep', 'wide'), 'narrow')
The draws below stay inside these ranges and needn't reach their ends.
All inputs are finite; a program needn't handle non-finite values.
Results may differ from the reference program's by a relative error of at most 0.023.
Values may be sent and summed in bfloat16 or wider, within the bound.
A program may use at most 64 MiB of HBM per device.

```python
import math
import jax
import jax.numpy as jnp
from jax import lax

D = 1280
FF = 4096
TOK = 256
SLOTS = 2
EXPERTS = 64
SLOT_ALL = 128
IMAGES = 256
N_NARROW = 8


def routing_values(key, lift_on):
    normal_key, scale_key, pick_key = jax.random.split(key, 3)
    normal_part = jnp.clip(jax.random.normal(normal_key, (D, SLOT_ALL), jnp.float32), -6.0, 6.0)
    column_scale = jnp.exp(jax.random.uniform(scale_key, (1, SLOT_ALL), jnp.float32, math.log(1.0), math.log(3.0)))
    picked = jax.random.permutation(pick_key, SLOT_ALL)[:4]
    marked = jnp.zeros((SLOT_ALL,), jnp.float32).at[picked].set(1.0)[None, :] * lift_on
    column_scale = column_scale * (1.0 - marked)
    values = jnp.clip(normal_part * column_scale * D ** (-0.5), -1.0, 1.0)
    return values


def draw_routing(key, part):
    lift_on = 0.0
    routing = routing_values(key, lift_on)
    return routing.astype(jnp.bfloat16)


def draw_tokens(key, part):
    key = jax.random.fold_in(key, 29)
    split_keys = jax.random.split(key, 2)
    row_scale = jnp.exp(jax.random.uniform(split_keys[1], (IMAGES, TOK, 1), jnp.float32, math.log(0.3), math.log(3.0)))
    values = jnp.clip(jax.random.normal(split_keys[0], (IMAGES, TOK, D), jnp.float32), -6.0, 6.0) * row_scale
    return jnp.clip(values, -24.0, 24.0).astype(jnp.bfloat16)


def levels(own_key, dims, cuts, low, high):
    def one(dim, shards_of):
        heights = jax.random.uniform(jax.random.fold_in(jax.random.fold_in(own_key, 6), dim), (shards_of,), jnp.float32, low / len(cuts), high / len(cuts))
        return jnp.repeat(jnp.exp(heights), dims[dim] // shards_of).reshape((-1,) + (1,) * (len(dims) - dim - 1))

    loudness = one(*cuts[0])
    for cut in cuts[1:]:
        loudness = loudness * one(*cut)
    return loudness


def bell_draw(key, extent, width, reach, cuts=(), held_as=jnp.bfloat16):
    gain = levels(key, extent, cuts, -0.22, 0.18) if cuts else 1.0
    array = jax.random.normal(key, extent, jnp.float32) * width * gain
    return jnp.minimum(jnp.maximum(array, -reach), reach).astype(held_as)


def setup_inputs(seed: int = 0) -> dict:
    arg_keys = jax.random.split(jax.random.key(seed), 7)
    tokens = draw_tokens(jax.random.fold_in(arg_keys[6], 71), 0)
    routing = draw_routing(jax.random.fold_in(arg_keys[6], 71), 0)
    grad_out = bell_draw(arg_keys[2], (IMAGES, TOK, D), 0.25, 1.5, ((0, 256),))
    slot_out = bell_draw(arg_keys[3], (IMAGES, SLOT_ALL, D), 1.0, 6.0, ((0, 256),))
    w_first = bell_draw(arg_keys[4], (EXPERTS, D, FF), D ** -0.5, 0.15625, ((0, 32), (2, 8)))
    w_second = bell_draw(arg_keys[5], (EXPERTS, FF, D), FF ** -0.5, 0.09375, ((0, 32), (1, 8)))
    return dict(tokens=tokens, routing=routing, grad_out=grad_out, slot_out=slot_out, w_first=w_first, w_second=w_second)


root_half = 0.7071067811865476
density_scale = 0.3989422804014327


def soft_max(values, over_dim):
    largest = jnp.max(values, axis=over_dim, keepdims=True)
    powers = jnp.exp(values - largest)
    return powers / jnp.sum(powers, axis=over_dim, keepdims=True)


def gelu_pair(hidden):
    normal_cdf = 0.5 * (1.0 + jax.scipy.special.erf(hidden * root_half))
    density = density_scale * jnp.exp(-0.5 * hidden * hidden)
    return hidden * normal_cdf, normal_cdf + hidden * density


def image_front(image_x, image_dy, routing):
    logits = jnp.dot(image_x, routing, preferred_element_type=jnp.float32)
    dispatch = soft_max(logits, 0)
    combine = soft_max(logits, 1)
    dispatch_bf = dispatch.astype(jnp.bfloat16)
    combine_bf = combine.astype(jnp.bfloat16)
    slot_in = jnp.dot(dispatch_bf.T, image_x, preferred_element_type=jnp.float32).astype(jnp.bfloat16)
    slot_grad = jnp.dot(combine_bf.T, image_dy, preferred_element_type=jnp.float32).astype(jnp.bfloat16)
    return dispatch, combine, slot_in, slot_grad


def expert_back(operands):
    rows_in, rows_grad, first_w, second_w = operands
    pre_act = jnp.dot(rows_in, first_w, preferred_element_type=jnp.float32)
    act_val, act_slope = gelu_pair(pre_act)
    act_bf = act_val.astype(jnp.bfloat16)
    act_grad = jnp.dot(rows_grad, second_w.T, preferred_element_type=jnp.float32)
    hid_grad = (act_grad * act_slope).astype(jnp.bfloat16)
    grad_second = jnp.dot(act_bf.T, rows_grad, preferred_element_type=jnp.float32).astype(jnp.bfloat16)
    grad_first = jnp.dot(rows_in.T, hid_grad, preferred_element_type=jnp.float32).astype(jnp.bfloat16)
    block_width = FF // N_NARROW
    blocks = jnp.einsum(
        "rbf,dbf->brd",
        hid_grad.astype(jnp.float32).reshape(-1, N_NARROW, block_width),
        first_w.astype(jnp.float32).reshape(-1, N_NARROW, block_width),
    )
    rounded = lax.optimization_barrier(blocks.astype(jnp.bfloat16))
    back_rows = jnp.sum(rounded.astype(jnp.float32), axis=0).astype(jnp.bfloat16)
    return grad_first, grad_second, back_rows


def image_back(image_x, image_dy, image_out, slot_back, dispatch, combine, routing):
    comb_raw = jnp.dot(image_dy, image_out.T, preferred_element_type=jnp.float32)
    logit_comb = combine * (comb_raw - jnp.sum(combine * comb_raw, axis=1, keepdims=True))
    disp_raw = jnp.dot(image_x, slot_back.T, preferred_element_type=jnp.float32)
    logit_disp = dispatch * (disp_raw - jnp.sum(dispatch * disp_raw, axis=0, keepdims=True))
    logit_grad = (logit_comb + logit_disp).astype(jnp.bfloat16)
    dispatch_bf = dispatch.astype(jnp.bfloat16)
    grad_x = (jnp.dot(logit_grad, routing.T, preferred_element_type=jnp.float32)
              + jnp.dot(dispatch_bf, slot_back, preferred_element_type=jnp.float32)).astype(jnp.bfloat16)
    routing_term = jnp.dot(image_x.T, logit_grad, preferred_element_type=jnp.float32)
    return grad_x, routing_term


def by_expert(slot_rows):
    return slot_rows.reshape(IMAGES, EXPERTS, SLOTS, D).transpose(1, 0, 2, 3).reshape(EXPERTS, IMAGES * SLOTS, D)


def reference(tokens, routing, grad_out, slot_out, w_first, w_second):
    dispatch, combine, slot_in, slot_grad = jax.vmap(image_front, in_axes=(0, 0, None))(tokens, grad_out, routing)
    grad_first, grad_second, back_rows = lax.map(
        expert_back, (by_expert(slot_in), by_expert(slot_grad), w_first, w_second))
    slot_back = back_rows.reshape(EXPERTS, IMAGES, SLOTS, D).transpose(1, 0, 2, 3).reshape(IMAGES, SLOT_ALL, D)
    grad_tokens, routing_terms = jax.vmap(image_back, in_axes=(0, 0, 0, 0, 0, 0, None))(
        tokens, grad_out, slot_out, slot_back, dispatch, combine, routing)
    grad_routing = jnp.sum(routing_terms, axis=0)
    return grad_tokens, grad_routing, grad_first, grad_second
```

```python
import functools

import jax
import jax.numpy as jnp
from jax import lax
from jax.experimental import pallas as pl
from jax.experimental.pallas import tpu as pltpu
from jax.sharding import PartitionSpec as P

MESH = pl.DeviceIdType.MESH
BF = jnp.bfloat16
F32 = jnp.float32
root_half = 0.7071067811865476
density_scale = 0.3989422804014327
D = 1280
HALF = 640


def nn(a, b):
    return lax.dot_general(a, b, (((1,), (0,)), ((), ())), preferred_element_type=F32)


def nt(a, b):
    return lax.dot_general(a, b, (((1,), (1,)), ((), ())), preferred_element_type=F32)


def tn(a, b):
    return lax.dot_general(a, b, (((0,), (0,)), ((), ())), preferred_element_type=F32)


def one_hot(rows, cols, pick):
    row = lax.broadcasted_iota(jnp.int32, (rows, cols), 0)
    col = lax.broadcasted_iota(jnp.int32, (rows, cols), 1)
    return (col == pick(row)).astype(F32).astype(BF)


def kernel(
    tok_h, routing_h, gout_h, sout_h, w1_h, w2_h,
    gx_h, gr_ref, g1_h, g2_h,
    tok, routing, gout, sout, w1, w2, gx, g1, g2,
    dispatch, combine, lcomb,
    zs, zr, ai, xg, rows, act, hid, pb, xr1, xr2, xs, yr, bb, zbs, zbr,
    rt, rr1, hh, rr2, gg, rr3, ex, rr4,
    ld_sem, out_sem, loc_sem,
    zf_s, zf_r, yi_s, yi_r, xi_s, xi_r, xg_s, xg_r, yg_s, yg_r,
    rx_s, rx_r, ry_s, ry_r, zb_s, zb_r,
    c_s, c_r, s2_s, s2_r, s3_s, s3_r, s4_s, s4_r,
):
    rep = lax.axis_index("rep")
    wide = lax.axis_index("wide")
    nar = lax.axis_index("narrow")
    x = nar % 4
    y = (nar // 4) * 2 + rep
    z = wide // 2
    c = wide % 2

    def dev_x(d):
        return (rep, wide, (nar // 4) * 4 + (x + d) % 4)

    def dev_y(d):
        yy = (y + d) % 4
        return (yy % 2, wide, (yy // 2) * 4 + x)

    def dev_w(k):
        return (rep, (wide + k) % 16, nar)

    core_dev = (rep, z * 2 + 1 - c, nar)

    def rc(src, dst, ss, rs, dev):
        return pltpu.make_async_remote_copy(
            src_ref=src, dst_ref=dst, send_sem=ss, recv_sem=rs, device_id=dev, device_id_type=MESH
        )

    pending = []

    def go(copy):
        copy.start()
        pending.append(copy)
        return copy

    loads = [
        pltpu.make_async_copy(h, v, ld_sem.at[i])
        for i, (h, v) in enumerate(
            ((tok_h.at[0], tok), (routing_h, routing), (gout_h.at[0], gout), (sout_h.at[0], sout), (w1_h, w1), (w2_h, w2))
        )
    ]
    for copy in loads:
        copy.start()

    barrier = pltpu.get_barrier_semaphore()

    def greet(dev):
        pl.semaphore_signal(barrier, inc=1, device_id=dev, device_id_type=MESH)

    @pl.loop(1, 16)
    def _(k):
        greet(dev_w(k))

    for d in (1, 2, 3):
        greet(dev_x(d))
        greet(dev_y(d))

    @pl.loop(0, 8)
    def _(k):
        @pl.when(jnp.logical_or(nar != z, k != z))
        def _():
            greet((rep, k * 2 + c, z))

    loads[0].wait()
    loads[1].wait()
    logits = nn(tok[...], routing[...])
    e0 = jnp.exp(logits - jnp.max(logits, axis=0, keepdims=True))
    dis = e0 / jnp.sum(e0, axis=0, keepdims=True)
    dispatch[...] = dis
    e1 = jnp.exp(logits - jnp.max(logits, axis=1, keepdims=True))
    com = e1 / jnp.sum(e1, axis=1, keepdims=True)
    combine[...] = com
    dis_bf = dis.astype(BF)
    com_bf = com.astype(BF)
    loads[2].wait()

    def z_copy(j, k):
        to = (wide + k) % 16
        return rc(zs.at[j, to], zr.at[j, wide], zf_s.at[j, k], zf_r.at[j, k], dev_w(k))

    for j in range(2):
        pt = one_hot(
            128, 128,
            lambda s: ((s >> 1) & 1) * 64 + (s >> 3) * 4 + j * 2 + (s & 1),
        )
        first = (lax.broadcasted_iota(jnp.int32, (128, HALF), 0) & 4) == 0
        parts = []
        for probs, src in ((dis_bf, tok), (com_bf, gout)):
            pick = nt(pt, probs).astype(BF)
            both = jnp.where(first, nn(pick, src[:, :HALF]), nn(pick, src[:, HALF:]))
            parts.append(both.reshape(16, 8, HALF))
        zs[j] = jnp.concatenate(parts, axis=1).astype(BF)
        if j == 0:
            pl.semaphore_wait(barrier, 15 + 6 + 7 + (nar != z).astype(jnp.int32))

        @pl.loop(1, 16)
        def _(k):
            z_copy(j, k).start()

        zr[j, wide] = zs[j, wide]

    def z_done(j):
        @pl.loop(1, 16)
        def _(k):
            z_copy(j, k).wait_recv()

    def spread(j):
        m = one_hot(
            256, 256,
            lambda r: ((r >> 1) & 15) * 16 + (r >> 7) * 8 + ((r >> 6) & 1) * 4 + ((r >> 5) & 1) * 2 + (r & 1),
        )
        out = nn(m, zr[j].reshape(256, HALF)).astype(BF)
        for h in range(2):
            cols = slice(h * HALF, (h + 1) * HALF)
            ai[j, :, :, cols] = out[h * 64:h * 64 + 64].reshape(2, 32, HALF)
            xg[j, x, :, :, cols] = out[128 + h * 64:128 + h * 64 + 64].reshape(2, 32, HALF)
        rows[j, 0, x, y] = ai[j, rep]

    def yin_send(j):
        return [
            go(rc(ai.at[j, (y + d) % 2], rows.at[j, 0, x, y], yi_s.at[j, d], yi_r.at[j, d], dev_y(d)))
            for d in (1, 3, 2)
        ]

    def xg_send(j):
        return [
            go(rc(xg.at[j, x], xg.at[j, x], xg_s.at[j, d], xg_r.at[j, d], dev_x(d)))
            for d in (1, 3)
        ]

    def xg_fwd(j):
        a, b = (x + 3) % 4, (x + 1) % 4
        return [
            go(rc(xg.at[j, a, 0], xg.at[j, a, 0], xg_s.at[j, 0], xg_r.at[j, 0], dev_x(1))),
            go(rc(xg.at[j, b, 1], xg.at[j, b, 1], xg_s.at[j, 2], xg_r.at[j, 2], dev_x(3))),
        ]

    def yg_send(j):
        out = [
            go(rc(xg.at[j, :, (y + d) % 2], rows.at[j, 1, :, y], yg_s.at[j, d], yg_r.at[j, d], dev_y(d)))
            for d in (1, 3, 2)
        ]
        own = pltpu.make_async_copy(xg.at[j, :, rep], rows.at[j, 1, :, y], loc_sem.at[j])
        own.start()
        return out, own

    def xin_send(j):
        return [
            go(rc(rows.at[j, 0, x], rows.at[j, 0, x], xi_s.at[j, d], xi_r.at[j, d], dev_x(d)))
            for d in (1, 3)
        ]

    def xin_fwd(j):
        a, b = (x + 3) % 4, (x + 1) % 4
        lo, hi = pl.ds(0, 2), pl.ds(2, 2)
        return [
            go(rc(rows.at[j, 0, a, lo], rows.at[j, 0, a, lo], xi_s.at[j, 0], xi_r.at[j, 0], dev_x(1))),
            go(rc(rows.at[j, 0, b, hi], rows.at[j, 0, b, hi], xi_s.at[j, 2], xi_r.at[j, 2], dev_x(3))),
        ]

    def arrive(copies):
        for copy in copies:
            copy.wait_recv()

    def hidden(j):
        @pl.loop(0, 2)
        def _(i):
            cols = pl.ds(pl.multiple_of(i * 256, 256), 256)
            pre = nn(rows[j, 0].reshape(512, D), w1[j, :, cols])
            cdf = 0.5 * (1.0 + lax.erf(pre * root_half))
            act[j, :, cols] = (pre * cdf).astype(BF)
            slope = cdf + pre * (density_scale * jnp.exp(-0.5 * pre * pre))
            grad = nt(rows[j, 1].reshape(512, D), w2[j, cols, :])
            hid[j, :, cols] = (grad * slope).astype(BF)

    def partial(j):
        @pl.loop(0, 5)
        def _(i):
            cols = pl.ds(pl.multiple_of(i * 256, 256), 256)
            pb[j, :, :, :, cols] = nt(hid[j], w1[j, cols, :]).astype(BF).reshape(4, 4, 32, 256)

    def grads(j):
        @pl.loop(0, 5)
        def _(i):
            cols = pl.ds(pl.multiple_of(i * 256, 256), 256)
            g1[j, cols, :] = tn(rows[j, 0, :, :, :, cols].reshape(512, 256), hid[j]).astype(BF)
            g2[j, :, cols] = tn(act[j], rows[j, 1, :, :, :, cols].reshape(512, 256)).astype(BF)
        a = pltpu.make_async_copy(g1.at[j], g1_h.at[j], out_sem.at[2 * j])
        b = pltpu.make_async_copy(g2.at[j], g2_h.at[j], out_sem.at[2 * j + 1])
        a.start()
        b.start()
        return [a, b]

    lo, hi = pl.ds(0, 2), pl.ds(2, 2)

    def xr_send(j):
        far, up, dn = (x + 2) % 4, (x + 1) % 4, (x + 3) % 4
        first = [
            go(rc(pb.at[j, far, lo], xr1.at[j, 0], rx_s.at[j, 0], rx_r.at[j, 0], dev_x(1))),
            go(rc(pb.at[j, far, hi], xr1.at[j, 1], rx_s.at[j, 1], rx_r.at[j, 1], dev_x(3))),
        ]
        second = [
            go(rc(pb.at[j, up, hi], xr2.at[j, 0, hi], rx_s.at[j, 2], rx_r.at[j, 2], dev_x(1))),
            go(rc(pb.at[j, dn, lo], xr2.at[j, 1, lo], rx_s.at[j, 3], rx_r.at[j, 3], dev_x(3))),
        ]
        return first, second

    def xr_fwd(j):
        up, dn = (x + 1) % 4, (x + 3) % 4
        pb[j, up, lo] = (pb[j, up, lo].astype(F32) + xr1[j, 0].astype(F32)).astype(BF)
        a = go(rc(pb.at[j, up, lo], xr2.at[j, 0, lo], rx_s.at[j, 4], rx_r.at[j, 4], dev_x(1)))
        pb[j, dn, hi] = (pb[j, dn, hi].astype(F32) + xr1[j, 1].astype(F32)).astype(BF)
        b = go(rc(pb.at[j, dn, hi], xr2.at[j, 1, hi], rx_s.at[j, 5], rx_r.at[j, 5], dev_x(3)))
        return [a, b]

    def yr_send(j):
        xs[j] = (pb[j, x].astype(F32) + xr2[j, 0].astype(F32) + xr2[j, 1].astype(F32)).astype(BF)
        return [
            go(rc(xs.at[j, (y + d) % 4], yr.at[j, d - 1], ry_s.at[j, d], ry_r.at[j, d], dev_y(d)))
            for d in (1, 3, 2)
        ]

    def yr_sum(j):
        bb[0, j] = (xs[j, y].astype(F32) + yr[j, 1].astype(F32)).astype(BF)
        bb[1, j] = (yr[j, 0].astype(F32) + yr[j, 2].astype(F32)).astype(BF)

    loads[3].wait()
    comb_raw = nt(gout[...], sout[...])
    com = combine[...]
    lcomb[...] = com * (comb_raw - jnp.sum(com * comb_raw, axis=1, keepdims=True))

    z_done(0)
    spread(0)
    yi0, xg0 = yin_send(0), xg_send(0)
    z_done(1)
    spread(1)
    arrive(xg0)
    xgf0 = xg_fwd(0)
    arrive(yi0)
    xi0 = xin_send(0)
    arrive(xgf0)
    yg0, own0 = yg_send(0)
    yi1, xg1 = yin_send(1), xg_send(1)
    arrive(xi0)
    xif0 = xin_fwd(0)
    arrive(xg1)
    xgf1 = xg_fwd(1)
    arrive(yi1)
    xi1 = xin_send(1)
    arrive(xgf1)
    yg1, own1 = yg_send(1)
    arrive(xif0)
    arrive(yg0)
    own0.wait()
    loads[4].wait()
    loads[5].wait()
    hidden(0)
    partial(0)
    rx0, rx0b = xr_send(0)
    arrive(xi1)
    xif1 = xin_fwd(1)
    out0 = grads(0)
    arrive(rx0)
    rxf0 = xr_fwd(0)
    arrive(xif1)
    arrive(yg1)
    own1.wait()
    hidden(1)
    partial(1)
    rx1, rx1b = xr_send(1)
    arrive(rx0b)
    arrive(rxf0)
    ry0 = yr_send(0)
    arrive(rx1)
    rxf1 = xr_fwd(1)
    out1 = grads(1)
    arrive(ry0)
    yr_sum(0)
    arrive(rx1b)
    arrive(rxf1)
    ry1 = yr_send(1)
    arrive(ry1)
    yr_sum(1)

    mb = one_hot(
        128, 128,
        lambda r: (((r >> 2) & 1) ^ rep) * 64 + ((r >> 1) & 1) * 32 + (r >> 3) * 2 + (r & 1),
    )
    back = nn(mb, bb[...].reshape(128, D)).reshape(16, 8, D)
    zbs[...] = jnp.concatenate([back[:, :, :HALF], back[:, :, HALF:]], axis=1).astype(BF)

    def zb_copy(k):
        to = (wide + k) % 16
        return rc(zbs.at[to], zbr.at[wide], zb_s.at[k], zb_r.at[k], dev_w(k))

    @pl.loop(1, 16)
    def _(k):
        zb_copy(k).start()

    zbr[wide] = zbs[wide]

    @pl.loop(1, 16)
    def _(k):
        zb_copy(k).wait_recv()

    recv = zbr[...].reshape(256, HALF)
    halves = []
    for h in range(2):
        q = one_hot(
            128, 256,
            lambda s: ((s >> 2) & 15) * 16 + h * 8 + (s >> 6) * 4 + (s & 3),
        )
        halves.append(nn(q, recv).astype(BF))
    slot_back = jnp.concatenate(halves, axis=1)
    disp_raw = nt(tok[...], slot_back)
    dis = dispatch[...]
    ldisp = dis * (disp_raw - jnp.sum(dis * disp_raw, axis=0, keepdims=True))
    lg = (lcomb[...] + ldisp).astype(BF)
    rt[...] = tn(tok[...], lg).reshape(16, 2, 40, 128)
    s1 = go(rc(rt.at[:, 1 - c], rr1, c_s, c_r, core_dev))
    gx[...] = (nt(lg, routing[...]) + nn(dis.astype(BF), slot_back)).astype(BF)
    outx = pltpu.make_async_copy(gx, gx_h.at[0], out_sem.at[4])
    outx.start()
    s1.wait_recv()
    hh[...] = (rt[:, c] + rr1[...]).reshape(4, 4, 40, 128)
    s2 = [
        go(rc(hh.at[:, (x + d) % 4], rr2.at[d - 1], s2_s.at[d], s2_r.at[d], dev_x(d)))
        for d in (1, 3, 2)
    ]
    arrive(s2)
    gg[...] = hh[:, x] + rr2[0] + rr2[1] + rr2[2]
    s3 = []
    for d in (1, 3, 2):
        yy = (y + d) % 4
        s3.append(
            go(rc(gg.at[(yy % 2) * 2 + yy // 2], rr3.at[d - 1], s3_s.at[d], s3_r.at[d], dev_y(d)))
        )
    arrive(s3)
    total = gg[(y % 2) * 2 + y // 2] + rr3[0] + rr3[1] + rr3[2]
    for i in range(8):
        ex[i, 0:5] = total[5 * i:5 * i + 5]

    def s4_copy(k):
        return rc(ex.at[k], rr4.at[z], s4_s.at[k], s4_r.at[z], (rep, nar * 2 + c, k))

    @pl.loop(0, 8)
    def _(k):
        own = jnp.logical_and(nar == z, k == nar)

        @pl.when(own)
        def _():
            rr4[z] = ex[k]

        @pl.when(jnp.logical_not(own))
        def _():
            s4_copy(k).start()

    @pl.loop(0, 8)
    def _(k):
        @pl.when(jnp.logical_not(jnp.logical_and(nar == z, k == z)))
        def _():
            rc(ex.at[0], rr4.at[k], s4_s.at[0], s4_r.at[k], core_dev).wait_recv()

    tot = rr4[0]
    for i in range(1, 8):
        tot = tot + rr4[i]
    gr_ref[...] = tot[0:5]

    @pl.loop(0, 8)
    def _(k):
        @pl.when(jnp.logical_not(jnp.logical_and(nar == z, k == nar)))
        def _():
            s4_copy(k).wait_send()

    @pl.loop(1, 16)
    def _(k):
        z_copy(0, k).wait_send()
        z_copy(1, k).wait_send()
        zb_copy(k).wait_send()

    for copy in pending:
        copy.wait_send()
    for copy in out0 + out1 + [outx]:
        copy.wait()


def local(tokens, routing, grad_out, slot_out, w_first, w_second):
    any_spec = pl.BlockSpec(memory_space=pl.ANY)
    v = pltpu.VMEM
    dma = pltpu.SemaphoreType.DMA
    return pl.pallas_call(
        kernel,
        out_shape=(
            jax.ShapeDtypeStruct((1, 256, D), BF),
            jax.ShapeDtypeStruct((5, 128), F32),
            jax.ShapeDtypeStruct((2, D, 512), BF),
            jax.ShapeDtypeStruct((2, 512, D), BF),
        ),
        in_specs=[any_spec] * 6,
        out_specs=(any_spec, pl.BlockSpec(memory_space=pltpu.VMEM), any_spec, any_spec),
        scratch_shapes=[
            v((256, D), BF), v((D, 128), BF), v((256, D), BF), v((128, D), BF),
            v((2, D, 512), BF), v((2, 512, D), BF),
            v((256, D), BF), v((2, D, 512), BF), v((2, 512, D), BF),
            v((256, 128), F32), v((256, 128), F32), v((256, 128), F32),
            v((2, 16, 16, HALF), BF), v((2, 16, 16, HALF), BF),
            v((2, 2, 32, D), BF), v((2, 4, 2, 32, D), BF), v((2, 2, 4, 4, 32, D), BF),
            v((2, 512, 512), BF), v((2, 512, 512), BF), v((2, 4, 4, 32, D), BF),
            v((2, 2, 2, 32, D), BF), v((2, 2, 4, 32, D), BF), v((2, 4, 32, D), BF),
            v((2, 3, 32, D), BF), v((2, 2, 32, D), BF), v((16, 16, HALF), BF), v((16, 16, HALF), BF),
            v((16, 2, 40, 128), F32), v((16, 40, 128), F32), v((4, 4, 40, 128), F32),
            v((3, 4, 40, 128), F32), v((4, 40, 128), F32), v((3, 40, 128), F32),
            v((8, 8, 128), F32), v((8, 8, 128), F32),
            dma((6,)), dma((5,)), dma((2,)),
            dma((2, 16)), dma((2, 16)), dma((2, 4)), dma((2, 4)), dma((2, 4)), dma((2, 4)),
            dma((2, 4)), dma((2, 4)), dma((2, 4)), dma((2, 4)),
            dma((2, 6)), dma((2, 6)), dma((2, 4)), dma((2, 4)), dma((16,)), dma((16,)),
            dma, dma, dma((4,)), dma((4,)), dma((4,)), dma((4,)), dma((8,)), dma((8,)),
        ],
        compiler_params=pltpu.CompilerParams(
            collective_id=0, has_side_effects=True, vmem_limit_bytes=56 * 2**20
        ),
    )(tokens, routing, grad_out, slot_out, w_first, w_second)


def solution(mesh):
    return jax.shard_map(
        local,
        mesh=mesh,
        in_specs=(
            P(("rep", "wide", "narrow"), None, None),
            P(),
            P(("rep", "wide", "narrow"), None, None),
            P(("rep", "wide", "narrow"), None, None),
            P(("rep", "wide"), None, "narrow"),
            P(("rep", "wide"), "narrow", None),
        ),
        out_specs=(
            P(("rep", "wide", "narrow"), None, None),
            P(("rep", "wide", "narrow"), None),
            P(("rep", "wide"), None, "narrow"),
            P(("rep", "wide"), "narrow", None),
        ),
        check_vma=False,
    )
```

```python
import functools

import jax
import jax.numpy as jnp
from jax import lax
from jax.experimental import pallas as pl
from jax.experimental.pallas import tpu as pltpu
from jax.sharding import PartitionSpec as P

MESH = pl.DeviceIdType.MESH
BF = jnp.bfloat16
F32 = jnp.float32
root_half = 0.7071067811865476
density_scale = 0.3989422804014327
D = 1280
HALF = 640
LIMIT = 56
OUT = pltpu.VMEM


def nn(a, b):
    return lax.dot_general(a, b, (((1,), (0,)), ((), ())), preferred_element_type=F32)


def nt(a, b):
    return lax.dot_general(a, b, (((1,), (1,)), ((), ())), preferred_element_type=F32)


def tn(a, b):
    return lax.dot_general(a, b, (((0,), (0,)), ((), ())), preferred_element_type=F32)


def one_hot(rows, cols, pick):
    row = lax.broadcasted_iota(jnp.int32, (rows, cols), 0)
    col = lax.broadcasted_iota(jnp.int32, (rows, cols), 1)
    return (col == pick(row)).astype(F32).astype(BF)


def kernel(
    tok_h, routing_h, gout_h, sout_h, w1_h, w2_h,
    gx, gr_ref, g1, g2,
    tok, routing, gout, sout, w1, w2,
    dispatch, combine, lcomb,
    zs, zr, ai, xg, rows, act, hid, pb, xr1, xr2, xs, yr, yq, qs, bb, zbs, zbr,
    tokt, rt, rr, ex, rr4,
    ld_sem, loc_sem,
    zf_s, zf_r, yi_s, yi_r, xi_s, xi_r, xg_s, xg_r, yg_s, yg_r,
    rx_s, rx_r, ry_s, ry_r, zb_s, zb_r,
    pl_s, pl_r, s4_s, s4_r,
):
    rep = lax.axis_index("rep")
    wide = lax.axis_index("wide")
    nar = lax.axis_index("narrow")
    x = nar % 4
    y = (nar // 4) * 2 + rep
    z = wide // 2
    c = wide % 2

    def dev_x(d):
        return (rep, wide, (nar // 4) * 4 + (x + d) % 4)

    def dev_y(d):
        yy = (y + d) % 4
        return (yy % 2, wide, (yy // 2) * 4 + x)

    def dev_w(k):
        return (rep, (wide + k) % 16, nar)

    core_dev = (rep, z * 2 + 1 - c, nar)

    def rc(src, dst, ss, rs, dev):
        return pltpu.make_async_remote_copy(
            src_ref=src, dst_ref=dst, send_sem=ss, recv_sem=rs, device_id=dev, device_id_type=MESH
        )

    pending = []

    def go(copy):
        copy.start()
        pending.append(copy)
        return copy

    loads = [
        pltpu.make_async_copy(h, v, ld_sem.at[i])
        for i, (h, v) in enumerate(
            ((tok_h.at[0], tok), (routing_h, routing), (gout_h.at[0], gout), (sout_h.at[0], sout), (w1_h, w1), (w2_h, w2))
        )
    ]
    for copy in loads[:4]:
        copy.start()

    barrier = pltpu.get_barrier_semaphore()

    def greet(dev):
        pl.semaphore_signal(barrier, inc=1, device_id=dev, device_id_type=MESH)

    @pl.loop(1, 16)
    def _(k):
        greet(dev_w(k))

    @pl.loop(1, 32)
    def _(k):
        cc, xx, yy = (c + k) % 2, (x + k // 2) % 4, (y + k // 8) % 4
        greet((yy % 2, z * 2 + cc, (yy // 2) * 4 + xx))

    @pl.loop(1, 8)
    def _(k):
        greet(dev_w(2 * k))

    loads[0].wait()
    loads[1].wait()
    logits = nn(tok[...], routing[...])
    e0 = jnp.exp(logits - jnp.max(logits, axis=0, keepdims=True))
    dis = e0 / jnp.sum(e0, axis=0, keepdims=True)
    dispatch[...] = dis
    e1 = jnp.exp(logits - jnp.max(logits, axis=1, keepdims=True))
    com = e1 / jnp.sum(e1, axis=1, keepdims=True)
    combine[...] = com
    dis_bf = dis.astype(BF)
    com_bf = com.astype(BF)
    loads[2].wait()
    loads[4].start()
    loads[5].start()

    def z_copy(kind, j, k):
        to = (wide + k) % 16
        return rc(
            zs.at[kind, j, to], zr.at[kind, j, wide], zf_s.at[kind, j, k], zf_r.at[kind, j, k], dev_w(k)
        )

    def z_pack(kind, j):
        pt = one_hot(
            128, 128,
            lambda s: ((s >> 1) & 1) * 64 + (s >> 3) * 4 + j * 2 + (s & 1),
        )
        first = (lax.broadcasted_iota(jnp.int32, (128, HALF), 0) & 4) == 0
        probs, src = ((dis_bf, tok), (com_bf, gout))[kind]
        pick = nt(pt, probs).astype(BF)
        both = jnp.where(first, nn(pick, src[:, :HALF]), nn(pick, src[:, HALF:]))
        zs[kind, j] = both.reshape(16, 8, HALF).astype(BF)

    def z_send(kind, j):
        @pl.loop(1, 16)
        def _(k):
            z_copy(kind, j, k).start()

        zr[kind, j, wide] = zs[kind, j, wide]

    def z_done(kind, j):
        @pl.loop(1, 16)
        def _(k):
            z_copy(kind, j, k).wait_recv()

    def spread(kind, j):
        m = one_hot(
            128, 128,
            lambda r: ((r >> 1) & 15) * 8 + (r >> 6) * 4 + ((r >> 5) & 1) * 2 + (r & 1),
        )
        out = nn(m, zr[kind, j].astype(F32).reshape(128, HALF).astype(BF)).astype(BF)
        for h in range(2):
            cols = slice(h * HALF, (h + 1) * HALF)
            part = out[h * 64:h * 64 + 64].reshape(2, 32, HALF)
            if kind == 0:
                ai[j, :, :, cols] = part
            else:
                xg[j, x, :, :, cols] = part
        if kind == 0:
            rows[j, 0, x, y] = ai[j, rep]

    z_pack(1, 0)
    pl.semaphore_wait(barrier, 15 + 31 + 7)
    z_send(1, 0)
    z_pack(0, 0)
    z_send(0, 0)
    z_pack(1, 1)
    z_pack(0, 1)

    def yin_send(j):
        return {
            d: go(rc(ai.at[j, (y + d) % 2], rows.at[j, 0, x, y], yi_s.at[j, d], yi_r.at[j, d], dev_y(d)))
            for d in (1, 3, 2)
        }

    def xin_copy(j, e, source, way, sem):
        block = rows.at[j, 0, source, (y + 4 - e) % 4]
        return go(rc(block, block, xi_s.at[j, e, sem], xi_r.at[j, e, sem], dev_x(way)))

    def xin_send(j, e):
        return [xin_copy(j, e, x, 1, 0), xin_copy(j, e, x, 3, 1)]

    def xin_fwd(j, e, direct):
        if e < 2:
            direct[0].wait_recv()
            return xin_copy(j, e, (x + 3) % 4, 1, 2)
        direct[1].wait_recv()
        return xin_copy(j, e, (x + 1) % 4, 3, 2)

    def xg_send(j):
        return [
            go(rc(xg.at[j, x], xg.at[j, x], xg_s.at[j, d], xg_r.at[j, d], dev_x(d)))
            for d in (1, 3)
        ]

    def xg_fwd(j):
        a, b = (x + 3) % 4, (x + 1) % 4
        return [
            go(rc(xg.at[j, a, 0], xg.at[j, a, 0], xg_s.at[j, 0], xg_r.at[j, 0], dev_x(1))),
            go(rc(xg.at[j, b, 1], xg.at[j, b, 1], xg_s.at[j, 2], xg_r.at[j, 2], dev_x(3))),
        ]

    def yg_send(j, e):
        source = (x + e) % 4
        own = pltpu.make_async_copy(xg.at[j, source, rep], rows.at[j, 1, source, y], loc_sem.at[j, e])
        own.start()
        out = [
            go(rc(xg.at[j, source, (y + d) % 2], rows.at[j, 1, source, y],
                  yg_s.at[j, e, d], yg_r.at[j, e, d], dev_y(d)))
            for d in (1, 3, 2)
        ]
        return out, own

    def arrive(copies):
        for copy in copies:
            copy.wait_recv()

    def hidden(j):
        @pl.loop(0, 2)
        def _(i):
            cols = pl.ds(pl.multiple_of(i * 256, 256), 256)
            pre = nn(rows[j, 0].reshape(512, D), w1[j, :, cols])
            cdf = 0.5 * (1.0 + lax.erf(pre * root_half))
            act[j, :, cols] = (pre * cdf).astype(BF)
            slope = cdf + pre * (density_scale * jnp.exp(-0.5 * pre * pre))
            grad = nt(rows[j, 1].reshape(512, D), w2[j, cols, :])
            hid[j, :, cols] = (grad * slope).astype(BF)

    def partial(j, h):
        @pl.loop(0, 5)
        def _(i):
            at = pl.ds(pl.multiple_of(h * HALF + i * 128, 128), 128)
            cols = pl.ds(pl.multiple_of(i * 128, 128), 128)
            pb[j, h, :, :, :, cols] = nt(hid[j], w1[j, at, :]).astype(BF).reshape(4, 4, 32, 128)

    def grads(j):
        @pl.loop(0, 5)
        def _(i):
            cols = pl.ds(pl.multiple_of(i * 256, 256), 256)
            g1[j, cols, :] = tn(rows[j, 0, :, :, :, cols].reshape(512, 256), hid[j]).astype(BF)
            g2[j, :, cols] = tn(act[j], rows[j, 1, :, :, :, cols].reshape(512, 256)).astype(BF)

    far, up, dn = (x + 2) % 4, (x + 1) % 4, (x + 3) % 4
    lo, hi = pl.ds(0, 2), pl.ds(2, 2)

    def add(*refs):
        total = refs[0][...].astype(F32)
        for ref in refs[1:]:
            total = total + ref[...].astype(F32)
        return total.astype(BF)

    def px_send(j, h):
        v = pb.at[j, h]
        return [
            go(rc(v.at[far, lo], xr1.at[j, h, 0], rx_s.at[j, h, 0], rx_r.at[j, h, 0], dev_x(1))),
            go(rc(v.at[far, hi], xr1.at[j, h, 1], rx_s.at[j, h, 1], rx_r.at[j, h, 1], dev_x(3))),
            go(rc(v.at[up, hi], xr2.at[j, h, 0, hi], rx_s.at[j, h, 2], rx_r.at[j, h, 2], dev_x(1))),
            go(rc(v.at[dn, lo], xr2.at[j, h, 1, lo], rx_s.at[j, h, 3], rx_r.at[j, h, 3], dev_x(3))),
        ]

    def px_fwd(j, h, sent):
        v = pb.at[j, h]
        sent[0].wait_recv()
        v[up, lo] = add(v.at[up, lo], xr1.at[j, h, 0])
        a = go(rc(v.at[up, lo], xr2.at[j, h, 0, lo], rx_s.at[j, h, 4], rx_r.at[j, h, 4], dev_x(1)))
        sent[1].wait_recv()
        v[dn, hi] = add(v.at[dn, hi], xr1.at[j, h, 1])
        b = go(rc(v.at[dn, hi], xr2.at[j, h, 1, hi], rx_s.at[j, h, 5], rx_r.at[j, h, 5], dev_x(3)))
        return [a, b, sent[2], sent[3]]

    def py_send(j, h, sent):
        arrive(sent)
        xs[j, h] = add(pb.at[j, h, x], xr2.at[j, h, 0], xr2.at[j, h, 1])
        return [
            go(rc(xs.at[j, h, (y + d) % 4], yr.at[j, h, d - 1], ry_s.at[j, h, d], ry_r.at[j, h, d], dev_y(d)))
            for d in (1, 3, 2)
        ]

    def p_sum(j, h, sent):
        arrive(sent)
        bb[j, h, 0] = add(xs.at[j, h, y], yr.at[j, h, 1])
        bb[j, h, 1] = add(yr.at[j, h, 0], yr.at[j, h, 2])

    def qy_send(j, h):
        return [
            go(rc(pb.at[j, h, :, (y + d) % 4], yq.at[d - 1], ry_s.at[j, h, d], ry_r.at[j, h, d], dev_y(d)))
            for d in (1, 3, 2)
        ]

    def qx_send(j, h, sent):
        arrive(sent)
        qs[0] = add(pb.at[j, h, :, y], yq.at[1])
        qs[1] = add(yq.at[0], yq.at[2])
        return [
            go(rc(qs.at[0, far], xr1.at[j, h, 0, 0], rx_s.at[j, h, 0], rx_r.at[j, h, 0], dev_x(1))),
            go(rc(qs.at[1, far], xr1.at[j, h, 1, 0], rx_s.at[j, h, 1], rx_r.at[j, h, 1], dev_x(3))),
            go(rc(qs.at[1, up], xr2.at[j, h, 0, 1], rx_s.at[j, h, 2], rx_r.at[j, h, 2], dev_x(1))),
            go(rc(qs.at[0, dn], xr2.at[j, h, 1, 0], rx_s.at[j, h, 3], rx_r.at[j, h, 3], dev_x(3))),
        ]

    def qx_fwd(j, h, sent):
        sent[0].wait_recv()
        qs[0, up] = add(qs.at[0, up], xr1.at[j, h, 0, 0])
        a = go(rc(qs.at[0, up], xr2.at[j, h, 0, 0], rx_s.at[j, h, 4], rx_r.at[j, h, 4], dev_x(1)))
        sent[1].wait_recv()
        qs[1, dn] = add(qs.at[1, dn], xr1.at[j, h, 1, 0])
        b = go(rc(qs.at[1, dn], xr2.at[j, h, 1, 1], rx_s.at[j, h, 5], rx_r.at[j, h, 5], dev_x(3)))
        return [a, b, sent[2], sent[3]]

    def q_sum(j, h, sent):
        arrive(sent)
        for o in range(2):
            bb[j, h, o] = add(qs.at[o, x], xr2.at[j, h, 0, o], xr2.at[j, h, 1, o])

    def zb_copy(j, k):
        to = (wide + k) % 16
        return rc(zbs.at[j, to], zbr.at[j, wide], zb_s.at[j, k], zb_r.at[j, k], dev_w(k))

    def zb_send(j):
        mb = one_hot(
            128, 64,
            lambda r: (((r >> 1) & 1) ^ rep) * 32 + (r >> 3) * 2 + (r & 1),
        )
        first = (lax.broadcasted_iota(jnp.int32, (128, HALF), 0) & 4) == 0
        both = [nn(mb, bb[j, h].reshape(64, HALF)) for h in range(2)]
        zbs[j] = jnp.where(first, both[0], both[1]).reshape(16, 8, HALF).astype(BF)

        @pl.loop(1, 16)
        def _(k):
            zb_copy(j, k).start()

        zbr[j, wide] = zbs[j, wide]

    def zb_done(j):
        @pl.loop(1, 16)
        def _(k):
            zb_copy(j, k).wait_recv()

    def turn():
        @pl.loop(0, 5)
        def _(i):
            row = lax.broadcasted_iota(jnp.int32, (256, D), 0) + i * 256
            col = lax.broadcasted_iota(jnp.int32, (256, D), 1)
            piece = (row * 52429) >> 18
            k = row - piece * 5
            zz, nn_, cc, lo_ = piece & 7, (piece >> 3) & 7, (piece >> 6) & 1, piece >> 7
            want = (((lo_ * 8 + zz) * 2 + cc) * 8 + nn_) * 5 + k
            pick = (col == want).astype(F32).astype(BF)
            tokt[pl.ds(pl.multiple_of(i * 256, 256), 256), :] = nt(pick, tok[...]).astype(BF)

    loads[3].wait()
    comb_raw = nt(gout[...], sout[...])
    com = combine[...]
    lcomb[...] = com * (comb_raw - jnp.sum(com * comb_raw, axis=1, keepdims=True))

    def step1(j, t):
        arrive(t["xg"])
        t["xgf"] = xg_fwd(j)
        t["yg"] += [yg_send(j, 3), yg_send(j, 1)]

    def step2(j, t):
        for d in (1, 3, 2):
            t["yi"][d].wait_recv()
            t["xi"][d] = xin_send(j, d)

    def step3(j, t):
        arrive(t["xgf"])
        t["yg"].append(yg_send(j, 2))

    def step4(j, t):
        for e in (0, 1, 3, 2):
            t["xf"].append(xin_fwd(j, e, t["xi"][e]))

    def step5(j, t):
        for e in (0, 1):
            t["xi"][e][1].wait_recv()
        for e in (2, 3):
            t["xi"][e][0].wait_recv()
        arrive(t["xf"])
        for out, own in t["yg"]:
            arrive(out)
            own.wait()

    def start_g(j):
        return dict(xg=xg_send(j), yg=[yg_send(j, 0)], xf=[])

    def start_i(j, t):
        t["yi"] = yin_send(j)
        t["xi"] = {0: xin_send(j, 0)}

    z_done(1, 0)
    z_send(1, 1)
    spread(1, 0)
    t0 = start_g(0)
    z_done(0, 0)
    z_send(0, 1)
    spread(0, 0)
    start_i(0, t0)
    turn()
    step1(0, t0)
    step2(0, t0)
    step3(0, t0)
    z_done(1, 1)
    spread(1, 1)
    z_done(0, 1)
    spread(0, 1)
    step4(0, t0)
    t1 = start_g(1)
    start_i(1, t1)
    loads[4].wait()
    loads[5].wait()
    step5(0, t0)
    hidden(0)
    step1(1, t1)
    step2(1, t1)
    partial(0, 0)
    partial(0, 1)
    step3(1, t1)
    step4(1, t1)
    p00 = px_send(0, 0)
    p01 = px_send(0, 1)
    step5(1, t1)
    hidden(1)
    p00 = px_fwd(0, 0, p00)
    p01 = px_fwd(0, 1, p01)
    partial(1, 1)
    q1 = qy_send(1, 1)
    partial(1, 0)
    p10 = px_send(1, 0)
    p00 = py_send(0, 0, p00)
    p01 = py_send(0, 1, p01)
    grads(0)
    q1 = qx_send(1, 1, q1)
    p10 = px_fwd(1, 0, p10)
    p_sum(0, 0, p00)
    p_sum(0, 1, p01)
    zb_send(0)
    q1 = qx_fwd(1, 1, q1)
    p10 = py_send(1, 0, p10)
    q_sum(1, 1, q1)
    p_sum(1, 0, p10)
    zb_send(1)
    grads(1)
    zb_done(0)
    zb_done(1)

    recv = zbr[...].astype(F32).reshape(256, HALF).astype(BF)
    halves = []
    for h in range(2):
        q = one_hot(
            128, 256,
            lambda s: ((s >> 1) & 1) * 128 + ((s >> 2) & 15) * 8 + h * 4 + (s >> 6) * 2 + (s & 1),
        )
        halves.append(nn(q, recv).astype(BF))
    slot_back = jnp.concatenate(halves, axis=1)
    disp_raw = nt(tok[...], slot_back)
    dis = dispatch[...]
    ldisp = dis * (disp_raw - jnp.sum(dis * disp_raw, axis=0, keepdims=True))
    lg = (lcomb[...] + ldisp).astype(BF)
    rt[...] = nn(tokt[...], lg).reshape(32, 40, 128).astype(BF)

    def plane_copy(k):
        cc, xx, yy = (c + k) % 2, (x + k // 2) % 4, (y + k // 8) % 4
        block = (yy % 2) * 16 + cc * 8 + (yy // 2) * 4 + xx
        dev = (yy % 2, z * 2 + cc, (yy // 2) * 4 + xx)
        return rc(rt.at[block], rr.at[k], pl_s.at[k], pl_r.at[k], dev)

    @pl.loop(1, 32)
    def _(k):
        plane_copy(k).start()

    rr[0] = rt[rep * 16 + c * 8 + nar]
    gx[0] = (nt(lg, routing[...]) + nn(dis.astype(BF), slot_back)).astype(BF)

    @pl.loop(1, 32)
    def _(k):
        plane_copy(k).wait_recv()

    total = jnp.sum(rr[...].astype(F32), axis=0)
    for i in range(8):
        ex[i, 0:5] = total[5 * i:5 * i + 5]

    def s4_copy(k):
        return rc(ex.at[(z + k) % 8], rr4.at[k], s4_s.at[k], s4_r.at[k], dev_w(2 * k))

    @pl.loop(1, 8)
    def _(k):
        s4_copy(k).start()

    rr4[0] = ex[z]

    @pl.loop(1, 8)
    def _(k):
        s4_copy(k).wait_recv()

    tot = rr4[0]
    for i in range(1, 8):
        tot = tot + rr4[i]
    gr_ref[...] = tot[0:5]

    @pl.loop(1, 8)
    def _(k):
        s4_copy(k).wait_send()

    @pl.loop(1, 16)
    def _(k):
        for j in range(2):
            z_copy(0, j, k).wait_send()
            z_copy(1, j, k).wait_send()
            zb_copy(j, k).wait_send()

    @pl.loop(1, 32)
    def _(k):
        plane_copy(k).wait_send()

    for copy in pending:
        copy.wait_send()


def local(tokens, routing, grad_out, slot_out, w_first, w_second):
    in_hbm = pl.BlockSpec(memory_space=pltpu.HBM)
    in_vmem = pl.BlockSpec(memory_space=pltpu.VMEM)
    v = pltpu.VMEM
    dma = pltpu.SemaphoreType.DMA
    shapes = (
        ((1, 256, D), BF),
        ((5, 128), F32),
        ((2, D, 512), BF),
        ((2, 512, D), BF),
    )
    return pl.pallas_call(
        kernel,
        out_shape=tuple(OUT(*shape) for shape in shapes),
        in_specs=[in_hbm] * 6,
        out_specs=(in_vmem,) * 4,
        scratch_shapes=[
            v((256, D), BF), v((D, 128), BF), v((256, D), BF), v((128, D), BF),
            v((2, D, 512), BF), v((2, 512, D), BF),
            v((256, 128), F32), v((256, 128), F32), v((256, 128), F32),
            v((2, 2, 16, 8, HALF), BF), v((2, 2, 16, 8, HALF), BF),
            v((2, 2, 32, D), BF), v((2, 4, 2, 32, D), BF), v((2, 2, 4, 4, 32, D), BF),
            v((2, 512, 512), BF), v((2, 512, 512), BF), v((2, 2, 4, 4, 32, HALF), BF),
            v((2, 2, 2, 2, 32, HALF), BF), v((2, 2, 2, 4, 32, HALF), BF), v((2, 2, 4, 32, HALF), BF),
            v((2, 2, 3, 32, HALF), BF), v((3, 4, 32, HALF), BF), v((2, 4, 32, HALF), BF),
            v((2, 2, 2, 32, HALF), BF),
            v((2, 16, 8, HALF), BF), v((2, 16, 8, HALF), BF),
            v((D, 256), BF), v((32, 40, 128), BF), v((32, 40, 128), BF),
            v((8, 8, 128), F32), v((8, 8, 128), F32),
            dma((6,)), dma((2, 4)),
            dma((2, 2, 16)), dma((2, 2, 16)), dma((2, 4)), dma((2, 4)), dma((2, 4, 3)), dma((2, 4, 3)),
            dma((2, 4)), dma((2, 4)), dma((2, 4, 4)), dma((2, 4, 4)),
            dma((2, 2, 6)), dma((2, 2, 6)), dma((2, 2, 4)), dma((2, 2, 4)), dma((2, 16)), dma((2, 16)),
            dma((32,)), dma((32,)), dma((8,)), dma((8,)),
        ],
        compiler_params=pltpu.CompilerParams(
            collective_id=0, has_side_effects=True, vmem_limit_bytes=LIMIT * 2**20
        ),
    )(tokens, routing, grad_out, slot_out, w_first, w_second)

def solution(mesh):
    return jax.shard_map(
        local,
        mesh=mesh,
        in_specs=(
            P(("rep", "wide", "narrow"), None, None),
            P(),
            P(("rep", "wide", "narrow"), None, None),
            P(("rep", "wide", "narrow"), None, None),
            P(("rep", "wide"), None, "narrow"),
            P(("rep", "wide"), "narrow", None),
        ),
        out_specs=(
            P(("rep", "wide", "narrow"), None, None),
            P(("rep", "wide", "narrow"), None),
            P(("rep", "wide"), None, "narrow"),
            P(("rep", "wide"), "narrow", None),
        ),
        check_vma=False,
    )
```

```python
import functools

import jax
import jax.numpy as jnp
from jax import lax
from jax.experimental import pallas as pl
from jax.experimental.pallas import tpu as pltpu
from jax.sharding import PartitionSpec as P

MESH = pl.DeviceIdType.MESH
BF = jnp.bfloat16
F32 = jnp.float32
root_half = 0.7071067811865476
density_scale = 0.3989422804014327
D = 1280
HALF = 640
LIMIT = 56
OUT = pltpu.VMEM


def nn(a, b):
    return lax.dot_general(a, b, (((1,), (0,)), ((), ())), preferred_element_type=F32)


def nt(a, b):
    return lax.dot_general(a, b, (((1,), (1,)), ((), ())), preferred_element_type=F32)


def tn(a, b):
    return lax.dot_general(a, b, (((0,), (0,)), ((), ())), preferred_element_type=F32)


def one_hot(rows, cols, pick):
    row = lax.broadcasted_iota(jnp.int32, (rows, cols), 0)
    col = lax.broadcasted_iota(jnp.int32, (rows, cols), 1)
    return (col == pick(row)).astype(F32).astype(BF)


def kernel(
    tok_h, routing_h, gout_h, sout_h, w1_h, w2_h,
    gx, gr_ref, g1, g2,
    tok, routing, gout, sout, w1, w2,
    dispatch, combine, lcomb,
    zs, zr, ai, xg, rows, act, hid, pb, xr1, xr2, xs, yr, yq, qs, bb, zbs, zbr,
    tokt, rt, rr, ex, rr4,
    ld_sem, loc_sem,
    zf_s, zf_r, yi_s, yi_r, xi_s, xi_r, xg_s, xg_r, yg_s, yg_r,
    rx_s, rx_r, ry_s, ry_r, zb_s, zb_r,
    pl_s, pl_r, s4_s, s4_r,
):
    rep = lax.axis_index("rep")
    wide = lax.axis_index("wide")
    nar = lax.axis_index("narrow")
    x = nar % 4
    y = (nar // 4) * 2 + rep
    z = wide // 2
    c = wide % 2

    def dev_x(d):
        return (rep, wide, (nar // 4) * 4 + (x + d) % 4)

    def dev_y(d):
        yy = (y + d) % 4
        return (yy % 2, wide, (yy // 2) * 4 + x)

    def dev_w(k):
        return (rep, (wide + k) % 16, nar)

    core_dev = (rep, z * 2 + 1 - c, nar)

    def rc(src, dst, ss, rs, dev):
        return pltpu.make_async_remote_copy(
            src_ref=src, dst_ref=dst, send_sem=ss, recv_sem=rs, device_id=dev, device_id_type=MESH
        )

    pending = []

    def go(copy):
        copy.start()
        pending.append(copy)
        return copy

    loads = [
        pltpu.make_async_copy(h, v, ld_sem.at[i])
        for i, (h, v) in enumerate(
            ((tok_h.at[0], tok), (routing_h, routing), (gout_h.at[0], gout), (sout_h.at[0], sout), (w1_h, w1), (w2_h, w2))
        )
    ]
    for copy in loads[:4]:
        copy.start()

    barrier = pltpu.get_barrier_semaphore()

    def greet(dev):
        pl.semaphore_signal(barrier, inc=1, device_id=dev, device_id_type=MESH)

    @pl.loop(1, 16)
    def _(k):
        greet(dev_w(k))

    @pl.loop(1, 32)
    def _(k):
        cc, xx, yy = (c + k) % 2, (x + k // 2) % 4, (y + k // 8) % 4
        greet((yy % 2, z * 2 + cc, (yy // 2) * 4 + xx))

    loads[0].wait()
    loads[1].wait()
    logits = nn(tok[...], routing[...])
    e0 = jnp.exp(logits - jnp.max(logits, axis=0, keepdims=True))
    dis = e0 / jnp.sum(e0, axis=0, keepdims=True)
    dispatch[...] = dis
    e1 = jnp.exp(logits - jnp.max(logits, axis=1, keepdims=True))
    com = e1 / jnp.sum(e1, axis=1, keepdims=True)
    combine[...] = com
    dis_bf = dis.astype(BF)
    com_bf = com.astype(BF)
    loads[2].wait()
    loads[4].start()
    loads[5].start()

    def z_copy(kind, j, k):
        to = (wide + k) % 16
        return rc(
            zs.at[kind, j, to], zr.at[kind, j, wide], zf_s.at[kind, j, k], zf_r.at[kind, j, k], dev_w(k)
        )

    def z_pack(kind, j):
        pt = one_hot(
            128, 128,
            lambda s: ((s >> 1) & 1) * 64 + (s >> 3) * 4 + j * 2 + (s & 1),
        )
        first = (lax.broadcasted_iota(jnp.int32, (128, HALF), 0) & 4) == 0
        probs, src = ((dis_bf, tok), (com_bf, gout))[kind]
        pick = nt(pt, probs).astype(BF)
        both = jnp.where(first, nn(pick, src[:, :HALF]), nn(pick, src[:, HALF:]))
        zs[kind, j] = both.reshape(16, 8, HALF).astype(BF)

    def z_send(kind, j):
        @pl.loop(1, 16)
        def _(k):
            z_copy(kind, j, k).start()

        zr[kind, j, wide] = zs[kind, j, wide]

    def z_done(kind, j):
        @pl.loop(1, 16)
        def _(k):
            z_copy(kind, j, k).wait_recv()

    def spread(kind, j):
        m = one_hot(
            128, 128,
            lambda r: ((r >> 1) & 15) * 8 + (r >> 6) * 4 + ((r >> 5) & 1) * 2 + (r & 1),
        )
        out = nn(m, zr[kind, j].astype(F32).reshape(128, HALF).astype(BF)).astype(BF)
        for h in range(2):
            cols = slice(h * HALF, (h + 1) * HALF)
            part = out[h * 64:h * 64 + 64].reshape(2, 32, HALF)
            if kind == 0:
                ai[j, :, :, cols] = part
            else:
                xg[j, x, :, :, cols] = part
        if kind == 0:
            rows[j, 0, x, y] = ai[j, rep]

    z_pack(1, 0)
    pl.semaphore_wait(barrier, 15 + 31)
    z_send(1, 0)
    z_pack(0, 0)
    z_send(0, 0)
    z_pack(1, 1)
    z_pack(0, 1)

    def yin_send(j):
        return {
            d: go(rc(ai.at[j, (y + d) % 2], rows.at[j, 0, x, y], yi_s.at[j, d], yi_r.at[j, d], dev_y(d)))
            for d in (1, 3, 2)
        }

    def xin_copy(j, e, source, way, sem):
        block = rows.at[j, 0, source, (y + 4 - e) % 4]
        return go(rc(block, block, xi_s.at[j, e, sem], xi_r.at[j, e, sem], dev_x(way)))

    def xin_send(j, e):
        return [xin_copy(j, e, x, 1, 0), xin_copy(j, e, x, 3, 1)]

    def xin_fwd(j, e, direct):
        if e < 2:
            direct[0].wait_recv()
            return xin_copy(j, e, (x + 3) % 4, 1, 2)
        direct[1].wait_recv()
        return xin_copy(j, e, (x + 1) % 4, 3, 2)

    def xg_send(j):
        return [
            go(rc(xg.at[j, x], xg.at[j, x], xg_s.at[j, d], xg_r.at[j, d], dev_x(d)))
            for d in (1, 3)
        ]

    def xg_fwd(j):
        a, b = (x + 3) % 4, (x + 1) % 4
        return [
            go(rc(xg.at[j, a, 0], xg.at[j, a, 0], xg_s.at[j, 0], xg_r.at[j, 0], dev_x(1))),
            go(rc(xg.at[j, b, 1], xg.at[j, b, 1], xg_s.at[j, 2], xg_r.at[j, 2], dev_x(3))),
        ]

    def yg_send(j, e):
        source = (x + e) % 4
        own = pltpu.make_async_copy(xg.at[j, source, rep], rows.at[j, 1, source, y], loc_sem.at[j, e])
        own.start()
        out = [
            go(rc(xg.at[j, source, (y + d) % 2], rows.at[j, 1, source, y],
                  yg_s.at[j, e, d], yg_r.at[j, e, d], dev_y(d)))
            for d in (1, 3, 2)
        ]
        return out, own

    def arrive(copies):
        for copy in copies:
            copy.wait_recv()

    def hidden(j):
        @pl.loop(0, 2)
        def _(i):
            cols = pl.ds(pl.multiple_of(i * 256, 256), 256)
            pre = nn(rows[j, 0].reshape(512, D), w1[j, :, cols])
            cdf = 0.5 * (1.0 + lax.erf(pre * root_half))
            act[j, :, cols] = (pre * cdf).astype(BF)
            slope = cdf + pre * (density_scale * jnp.exp(-0.5 * pre * pre))
            grad = nt(rows[j, 1].reshape(512, D), w2[j, cols, :])
            hid[j, :, cols] = (grad * slope).astype(BF)

    def partial(j, h):
        @pl.loop(0, 5)
        def _(i):
            at = pl.ds(pl.multiple_of(h * HALF + i * 128, 128), 128)
            cols = pl.ds(pl.multiple_of(i * 128, 128), 128)
            pb[j, h, :, :, :, cols] = nt(hid[j], w1[j, at, :]).astype(BF).reshape(4, 4, 32, 128)

    def grads(j):
        @pl.loop(0, 5)
        def _(i):
            cols = pl.ds(pl.multiple_of(i * 256, 256), 256)
            g1[j, cols, :] = tn(rows[j, 0, :, :, :, cols].reshape(512, 256), hid[j]).astype(BF)
            g2[j, :, cols] = tn(act[j], rows[j, 1, :, :, :, cols].reshape(512, 256)).astype(BF)

    far, up, dn = (x + 2) % 4, (x + 1) % 4, (x + 3) % 4
    lo, hi = pl.ds(0, 2), pl.ds(2, 2)

    def add(*refs):
        total = refs[0][...].astype(F32)
        for ref in refs[1:]:
            total = total + ref[...].astype(F32)
        return total.astype(BF)

    def px_send(j, h):
        v = pb.at[j, h]
        return [
            go(rc(v.at[far, lo], xr1.at[j, h, 0], rx_s.at[j, h, 0], rx_r.at[j, h, 0], dev_x(1))),
            go(rc(v.at[far, hi], xr1.at[j, h, 1], rx_s.at[j, h, 1], rx_r.at[j, h, 1], dev_x(3))),
            go(rc(v.at[up, hi], xr2.at[j, h, 0, hi], rx_s.at[j, h, 2], rx_r.at[j, h, 2], dev_x(1))),
            go(rc(v.at[dn, lo], xr2.at[j, h, 1, lo], rx_s.at[j, h, 3], rx_r.at[j, h, 3], dev_x(3))),
        ]

    def px_fwd(j, h, sent):
        v = pb.at[j, h]
        sent[0].wait_recv()
        v[up, lo] = add(v.at[up, lo], xr1.at[j, h, 0])
        a = go(rc(v.at[up, lo], xr2.at[j, h, 0, lo], rx_s.at[j, h, 4], rx_r.at[j, h, 4], dev_x(1)))
        sent[1].wait_recv()
        v[dn, hi] = add(v.at[dn, hi], xr1.at[j, h, 1])
        b = go(rc(v.at[dn, hi], xr2.at[j, h, 1, hi], rx_s.at[j, h, 5], rx_r.at[j, h, 5], dev_x(3)))
        return [a, b, sent[2], sent[3]]

    def py_send(j, h, sent):
        arrive(sent)
        xs[j, h] = add(pb.at[j, h, x], xr2.at[j, h, 0], xr2.at[j, h, 1])
        return [
            go(rc(xs.at[j, h, (y + d) % 4], yr.at[j, h, d - 1], ry_s.at[j, h, d], ry_r.at[j, h, d], dev_y(d)))
            for d in (1, 3, 2)
        ]

    def p_sum(j, h, sent):
        arrive(sent)
        bb[j, h, 0] = add(xs.at[j, h, y], yr.at[j, h, 1])
        bb[j, h, 1] = add(yr.at[j, h, 0], yr.at[j, h, 2])

    def qy_send(j, h):
        return [
            go(rc(pb.at[j, h, :, (y + d) % 4], yq.at[d - 1], ry_s.at[j, h, d], ry_r.at[j, h, d], dev_y(d)))
            for d in (1, 3, 2)
        ]

    def qx_send(j, h, sent):
        arrive(sent)
        qs[0] = add(pb.at[j, h, :, y], yq.at[1])
        qs[1] = add(yq.at[0], yq.at[2])
        return [
            go(rc(qs.at[0, far], xr1.at[j, h, 0, 0], rx_s.at[j, h, 0], rx_r.at[j, h, 0], dev_x(1))),
            go(rc(qs.at[1, far], xr1.at[j, h, 1, 0], rx_s.at[j, h, 1], rx_r.at[j, h, 1], dev_x(3))),
            go(rc(qs.at[1, up], xr2.at[j, h, 0, 1], rx_s.at[j, h, 2], rx_r.at[j, h, 2], dev_x(1))),
            go(rc(qs.at[0, dn], xr2.at[j, h, 1, 0], rx_s.at[j, h, 3], rx_r.at[j, h, 3], dev_x(3))),
        ]

    def qx_fwd(j, h, sent):
        sent[0].wait_recv()
        qs[0, up] = add(qs.at[0, up], xr1.at[j, h, 0, 0])
        a = go(rc(qs.at[0, up], xr2.at[j, h, 0, 0], rx_s.at[j, h, 4], rx_r.at[j, h, 4], dev_x(1)))
        sent[1].wait_recv()
        qs[1, dn] = add(qs.at[1, dn], xr1.at[j, h, 1, 0])
        b = go(rc(qs.at[1, dn], xr2.at[j, h, 1, 1], rx_s.at[j, h, 5], rx_r.at[j, h, 5], dev_x(3)))
        return [a, b, sent[2], sent[3]]

    def q_sum(j, h, sent):
        arrive(sent)
        for o in range(2):
            bb[j, h, o] = add(qs.at[o, x], xr2.at[j, h, 0, o], xr2.at[j, h, 1, o])

    def zb_copy(j, k):
        to = (wide + k) % 16
        return rc(zbs.at[j, to], zbr.at[j, wide], zb_s.at[j, k], zb_r.at[j, k], dev_w(k))

    def zb_send(j):
        mb = one_hot(
            128, 64,
            lambda r: (((r >> 1) & 1) ^ rep) * 32 + (r >> 3) * 2 + (r & 1),
        )
        first = (lax.broadcasted_iota(jnp.int32, (128, HALF), 0) & 4) == 0
        both = [nn(mb, bb[j, h].reshape(64, HALF)) for h in range(2)]
        zbs[j] = jnp.where(first, both[0], both[1]).reshape(16, 8, HALF).astype(BF)

        @pl.loop(1, 16)
        def _(k):
            zb_copy(j, k).start()

        zbr[j, wide] = zbs[j, wide]

    def zb_done(j):
        @pl.loop(1, 16)
        def _(k):
            zb_copy(j, k).wait_recv()

    def turn():
        @pl.loop(0, 5)
        def _(i):
            row = lax.broadcasted_iota(jnp.int32, (256, D), 0) + i * 256
            col = lax.broadcasted_iota(jnp.int32, (256, D), 1)
            piece = (row * 52429) >> 18
            k = row - piece * 5
            zz, nn_, cc, lo_ = piece & 7, (piece >> 3) & 7, (piece >> 6) & 1, piece >> 7
            want = (((lo_ * 8 + zz) * 2 + cc) * 8 + nn_) * 5 + k
            pick = (col == want).astype(F32).astype(BF)
            tokt[pl.ds(pl.multiple_of(i * 256, 256), 256), :] = nt(pick, tok[...]).astype(BF)

    loads[3].wait()
    comb_raw = nt(gout[...], sout[...])
    com = combine[...]
    lcomb[...] = com * (comb_raw - jnp.sum(com * comb_raw, axis=1, keepdims=True))

    def step1(j, t):
        arrive(t["xg"])
        t["xgf"] = xg_fwd(j)
        t["yg"] += [yg_send(j, 3), yg_send(j, 1)]

    def step2(j, t):
        for d in (1, 3, 2):
            t["yi"][d].wait_recv()
            t["xi"][d] = xin_send(j, d)

    def step3(j, t):
        arrive(t["xgf"])
        t["yg"].append(yg_send(j, 2))

    def step4(j, t):
        for e in (0, 1, 3, 2):
            t["xf"].append(xin_fwd(j, e, t["xi"][e]))

    def step5(j, t):
        for e in (0, 1):
            t["xi"][e][1].wait_recv()
        for e in (2, 3):
            t["xi"][e][0].wait_recv()
        arrive(t["xf"])
        for out, own in t["yg"]:
            arrive(out)
            own.wait()

    def start_g(j):
        return dict(xg=xg_send(j), yg=[yg_send(j, 0)], xf=[])

    def start_i(j, t):
        t["yi"] = yin_send(j)
        t["xi"] = {0: xin_send(j, 0)}

    z_done(1, 0)
    z_send(1, 1)
    spread(1, 0)
    t0 = start_g(0)
    z_done(0, 0)
    z_send(0, 1)
    spread(0, 0)
    start_i(0, t0)
    turn()
    step1(0, t0)
    step2(0, t0)
    step3(0, t0)
    z_done(1, 1)
    spread(1, 1)
    z_done(0, 1)
    spread(0, 1)
    step4(0, t0)
    t1 = start_g(1)
    start_i(1, t1)
    loads[4].wait()
    loads[5].wait()
    step5(0, t0)
    hidden(0)
    step1(1, t1)
    step2(1, t1)
    partial(0, 0)
    partial(0, 1)
    step3(1, t1)
    step4(1, t1)
    p00 = px_send(0, 0)
    p01 = px_send(0, 1)
    step5(1, t1)
    hidden(1)
    partial(1, 1)
    q1 = qy_send(1, 1)
    p00 = px_fwd(0, 0, p00)
    p01 = px_fwd(0, 1, p01)
    partial(1, 0)
    p10 = px_send(1, 0)
    p00 = py_send(0, 0, p00)
    p01 = py_send(0, 1, p01)
    q1 = qx_send(1, 1, q1)
    p10 = px_fwd(1, 0, p10)
    p_sum(0, 0, p00)
    p_sum(0, 1, p01)
    zb_send(0)
    q1 = qx_fwd(1, 1, q1)
    p10 = py_send(1, 0, p10)
    q_sum(1, 1, q1)
    p_sum(1, 0, p10)
    zb_send(1)
    grads(0)
    grads(1)
    zb_done(0)
    zb_done(1)

    recv = zbr[...].astype(F32).reshape(256, HALF).astype(BF)
    halves = []
    for h in range(2):
        q = one_hot(
            128, 256,
            lambda s: ((s >> 1) & 1) * 128 + ((s >> 2) & 15) * 8 + h * 4 + (s >> 6) * 2 + (s & 1),
        )
        halves.append(nn(q, recv).astype(BF))
    slot_back = jnp.concatenate(halves, axis=1)
    disp_raw = nt(tok[...], slot_back)
    dis = dispatch[...]
    ldisp = dis * (disp_raw - jnp.sum(dis * disp_raw, axis=0, keepdims=True))
    lg = (lcomb[...] + ldisp).astype(BF)
    rt[...] = nn(tokt[...], lg).reshape(32, 40, 128).astype(BF)

    def plane_copy(k):
        cc, xx, yy = (c + k) % 2, (x + k // 2) % 4, (y + k // 8) % 4
        block = (yy % 2) * 16 + cc * 8 + (yy // 2) * 4 + xx
        dev = (yy % 2, z * 2 + cc, (yy // 2) * 4 + xx)
        return rc(rt.at[block], rr.at[k], pl_s.at[k], pl_r.at[k], dev)

    @pl.loop(1, 32)
    def _(k):
        plane_copy(k).start()

    rr[0] = rt[rep * 16 + c * 8 + nar]
    gx[0] = (nt(lg, routing[...]) + nn(dis.astype(BF), slot_back)).astype(BF)

    @pl.loop(1, 32)
    def _(k):
        plane_copy(k).wait_recv()

    total = jnp.sum(rr[...].astype(F32), axis=0)
    for i in range(8):
        ex[i, 0:5] = total[5 * i:5 * i + 5]

    def s4_copy(k):
        return rc(ex.at[(z + k) % 8], rr4.at[k], s4_s.at[k], s4_r.at[k], dev_w(2 * k))

    @pl.loop(1, 8)
    def _(k):
        s4_copy(k).start()

    rr4[0] = ex[z]

    @pl.loop(1, 8)
    def _(k):
        s4_copy(k).wait_recv()

    tot = rr4[0]
    for i in range(1, 8):
        tot = tot + rr4[i]
    gr_ref[...] = tot[0:5]

    @pl.loop(1, 8)
    def _(k):
        s4_copy(k).wait_send()

    @pl.loop(1, 16)
    def _(k):
        for j in range(2):
            z_copy(0, j, k).wait_send()
            z_copy(1, j, k).wait_send()
            zb_copy(j, k).wait_send()

    @pl.loop(1, 32)
    def _(k):
        plane_copy(k).wait_send()

    for copy in pending:
        copy.wait_send()


def local(tokens, routing, grad_out, slot_out, w_first, w_second):
    in_hbm = pl.BlockSpec(memory_space=pltpu.HBM)
    in_vmem = pl.BlockSpec(memory_space=pltpu.VMEM)
    v = pltpu.VMEM
    dma = pltpu.SemaphoreType.DMA
    shapes = (
        ((1, 256, D), BF),
        ((5, 128), F32),
        ((2, D, 512), BF),
        ((2, 512, D), BF),
    )
    return pl.pallas_call(
        kernel,
        out_shape=tuple(OUT(*shape) for shape in shapes),
        in_specs=[in_hbm] * 6,
        out_specs=(in_vmem,) * 4,
        scratch_shapes=[
            v((256, D), BF), v((D, 128), BF), v((256, D), BF), v((128, D), BF),
            v((2, D, 512), BF), v((2, 512, D), BF),
            v((256, 128), F32), v((256, 128), F32), v((256, 128), F32),
            v((2, 2, 16, 8, HALF), BF), v((2, 2, 16, 8, HALF), BF),
            v((2, 2, 32, D), BF), v((2, 4, 2, 32, D), BF), v((2, 2, 4, 4, 32, D), BF),
            v((2, 512, 512), BF), v((2, 512, 512), BF), v((2, 2, 4, 4, 32, HALF), BF),
            v((2, 2, 2, 2, 32, HALF), BF), v((2, 2, 2, 4, 32, HALF), BF), v((2, 2, 4, 32, HALF), BF),
            v((2, 2, 3, 32, HALF), BF), v((3, 4, 32, HALF), BF), v((2, 4, 32, HALF), BF),
            v((2, 2, 2, 32, HALF), BF),
            v((2, 16, 8, HALF), BF), v((2, 16, 8, HALF), BF),
            v((D, 256), BF), v((32, 40, 128), BF), v((32, 40, 128), BF),
            v((8, 8, 128), F32), v((8, 8, 128), F32),
            dma((6,)), dma((2, 4)),
            dma((2, 2, 16)), dma((2, 2, 16)), dma((2, 4)), dma((2, 4)), dma((2, 4, 3)), dma((2, 4, 3)),
            dma((2, 4)), dma((2, 4)), dma((2, 4, 4)), dma((2, 4, 4)),
            dma((2, 2, 6)), dma((2, 2, 6)), dma((2, 2, 4)), dma((2, 2, 4)), dma((2, 16)), dma((2, 16)),
            dma((32,)), dma((32,)), dma((8,)), dma((8,)),
        ],
        compiler_params=pltpu.CompilerParams(
            collective_id=0, has_side_effects=True, vmem_limit_bytes=LIMIT * 2**20
        ),
    )(tokens, routing, grad_out, slot_out, w_first, w_second)

def solution(mesh):
    return jax.shard_map(
        local,
        mesh=mesh,
        in_specs=(
            P(("rep", "wide", "narrow"), None, None),
            P(),
            P(("rep", "wide", "narrow"), None, None),
            P(("rep", "wide", "narrow"), None, None),
            P(("rep", "wide"), None, "narrow"),
            P(("rep", "wide"), "narrow", None),
        ),
        out_specs=(
            P(("rep", "wide", "narrow"), None, None),
            P(("rep", "wide", "narrow"), None),
            P(("rep", "wide"), None, "narrow"),
            P(("rep", "wide"), "narrow", None),
        ),
        check_vma=False,
    )
```

```python
import functools

import jax
import jax.numpy as jnp
from jax import lax
from jax.experimental import pallas as pl
from jax.experimental.pallas import tpu as pltpu
from jax.sharding import PartitionSpec as P

MESH = pl.DeviceIdType.MESH
BF = jnp.bfloat16
F32 = jnp.float32
root_half = 0.7071067811865476
density_scale = 0.3989422804014327
D = 1280
HALF = 640
LIMIT = 56
OUT = pltpu.VMEM


def nn(a, b):
    return lax.dot_general(a, b, (((1,), (0,)), ((), ())), preferred_element_type=F32)


def nt(a, b):
    return lax.dot_general(a, b, (((1,), (1,)), ((), ())), preferred_element_type=F32)


def tn(a, b):
    return lax.dot_general(a, b, (((0,), (0,)), ((), ())), preferred_element_type=F32)


def one_hot(rows, cols, pick):
    row = lax.broadcasted_iota(jnp.int32, (rows, cols), 0)
    col = lax.broadcasted_iota(jnp.int32, (rows, cols), 1)
    return (col == pick(row)).astype(F32).astype(BF)


def kernel(
    tok_h, routing_h, gout_h, sout_h, w1_h, w2_h,
    gx, gr_ref, g1, g2,
    tok, routing, gout, sout, w1, w2,
    dispatch, combine, lcomb,
    zs, zr, ai, xg, rows, act, hid, pb, xr1, xr2, xs, yr, yq, qs, bb, zbs, zbr,
    tokt, rt, rr, ex, rr4,
    ld_sem, loc_sem,
    zf_s, zf_r, yi_s, yi_r, xi_s, xi_r, xg_s, xg_r, yg_s, yg_r,
    rx_s, rx_r, ry_s, ry_r, zb_s, zb_r,
    pl_s, pl_r, s4_s, s4_r,
):
    rep = lax.axis_index("rep")
    wide = lax.axis_index("wide")
    nar = lax.axis_index("narrow")
    x = nar % 4
    y = (nar // 4) * 2 + rep
    z = wide // 2
    c = wide % 2

    def dev_x(d):
        return (rep, wide, (nar // 4) * 4 + (x + d) % 4)

    def dev_y(d):
        yy = (y + d) % 4
        return (yy % 2, wide, (yy // 2) * 4 + x)

    def dev_w(k):
        return (rep, (wide + k) % 16, nar)

    core_dev = (rep, z * 2 + 1 - c, nar)

    def rc(src, dst, ss, rs, dev):
        return pltpu.make_async_remote_copy(
            src_ref=src, dst_ref=dst, send_sem=ss, recv_sem=rs, device_id=dev, device_id_type=MESH
        )

    pending = []

    def go(copy):
        copy.start()
        pending.append(copy)
        return copy

    loads = [
        pltpu.make_async_copy(h, v, ld_sem.at[i])
        for i, (h, v) in enumerate(
            ((tok_h.at[0], tok), (routing_h, routing), (gout_h.at[0], gout), (sout_h.at[0], sout), (w1_h, w1), (w2_h, w2))
        )
    ]
    for copy in loads[:4]:
        copy.start()

    barrier = pltpu.get_barrier_semaphore()

    def greet(dev):
        pl.semaphore_signal(barrier, inc=1, device_id=dev, device_id_type=MESH)

    @pl.loop(1, 16)
    def _(k):
        greet(dev_w(k))

    @pl.loop(1, 32)
    def _(k):
        cc, xx, yy = (c + k) % 2, (x + k // 2) % 4, (y + k // 8) % 4
        greet((yy % 2, z * 2 + cc, (yy // 2) * 4 + xx))

    loads[0].wait()
    loads[1].wait()
    logits = nn(tok[...], routing[...])
    e0 = jnp.exp(logits - jnp.max(logits, axis=0, keepdims=True))
    dis = e0 / jnp.sum(e0, axis=0, keepdims=True)
    dispatch[...] = dis
    e1 = jnp.exp(logits - jnp.max(logits, axis=1, keepdims=True))
    com = e1 / jnp.sum(e1, axis=1, keepdims=True)
    combine[...] = com
    dis_bf = dis.astype(BF)
    com_bf = com.astype(BF)
    loads[2].wait()
    loads[4].start()
    loads[5].start()

    def z_copy(kind, j, k):
        to = (wide + k) % 16
        return rc(
            zs.at[kind, j, to], zr.at[kind, j, wide], zf_s.at[kind, j, k], zf_r.at[kind, j, k], dev_w(k)
        )

    def z_pack(kind, j):
        pt = one_hot(
            128, 128,
            lambda s: ((s >> 1) & 1) * 64 + (s >> 3) * 4 + j * 2 + (s & 1),
        )
        first = (lax.broadcasted_iota(jnp.int32, (128, HALF), 0) & 4) == 0
        probs, src = ((dis_bf, tok), (com_bf, gout))[kind]
        pick = nt(pt, probs).astype(BF)
        both = jnp.where(first, nn(pick, src[:, :HALF]), nn(pick, src[:, HALF:]))
        zs[kind, j] = both.reshape(16, 8, HALF).astype(BF)

    def z_send(kind, j):
        @pl.loop(1, 16)
        def _(k):
            z_copy(kind, j, k).start()

        zr[kind, j, wide] = zs[kind, j, wide]

    def z_done(kind, j):
        @pl.loop(1, 16)
        def _(k):
            z_copy(kind, j, k).wait_recv()

    def spread(kind, j):
        m = one_hot(
            128, 128,
            lambda r: ((r >> 1) & 15) * 8 + (r >> 6) * 4 + ((r >> 5) & 1) * 2 + (r & 1),
        )
        out = nn(m, zr[kind, j].astype(F32).reshape(128, HALF).astype(BF)).astype(BF)
        for h in range(2):
            cols = slice(h * HALF, (h + 1) * HALF)
            part = out[h * 64:h * 64 + 64].reshape(2, 32, HALF)
            if kind == 0:
                ai[j, :, :, cols] = part
            else:
                xg[j, x, :, :, cols] = part
        if kind == 0:
            rows[j, 0, x, y] = ai[j, rep]

    z_pack(1, 0)
    pl.semaphore_wait(barrier, 15 + 31)
    z_send(1, 0)
    z_pack(0, 0)
    z_send(0, 0)
    z_pack(1, 1)
    z_pack(0, 1)

    def yin_send(j):
        return {
            d: go(rc(ai.at[j, (y + d) % 2], rows.at[j, 0, x, y], yi_s.at[j, d], yi_r.at[j, d], dev_y(d)))
            for d in (1, 3, 2)
        }

    def xin_copy(j, e, source, way, sem):
        block = rows.at[j, 0, source, (y + 4 - e) % 4]
        return go(rc(block, block, xi_s.at[j, e, sem], xi_r.at[j, e, sem], dev_x(way)))

    def xin_send(j, e):
        return [xin_copy(j, e, x, 1, 0), xin_copy(j, e, x, 3, 1)]

    def xin_fwd(j, e, direct):
        if e < 2:
            direct[0].wait_recv()
            return xin_copy(j, e, (x + 3) % 4, 1, 2)
        direct[1].wait_recv()
        return xin_copy(j, e, (x + 1) % 4, 3, 2)

    def xg_send(j):
        return [
            go(rc(xg.at[j, x], xg.at[j, x], xg_s.at[j, d], xg_r.at[j, d], dev_x(d)))
            for d in (1, 3)
        ]

    def xg_fwd(j):
        a, b = (x + 3) % 4, (x + 1) % 4
        return [
            go(rc(xg.at[j, a, 0], xg.at[j, a, 0], xg_s.at[j, 0], xg_r.at[j, 0], dev_x(1))),
            go(rc(xg.at[j, b, 1], xg.at[j, b, 1], xg_s.at[j, 2], xg_r.at[j, 2], dev_x(3))),
        ]

    def yg_send(j, e):
        source = (x + e) % 4
        own = pltpu.make_async_copy(xg.at[j, source, rep], rows.at[j, 1, source, y], loc_sem.at[j, e])
        own.start()
        out = [
            go(rc(xg.at[j, source, (y + d) % 2], rows.at[j, 1, source, y],
                  yg_s.at[j, e, d], yg_r.at[j, e, d], dev_y(d)))
            for d in (1, 3, 2)
        ]
        return out, own

    def arrive(copies):
        for copy in copies:
            copy.wait_recv()

    def hidden(j):
        @pl.loop(0, 2)
        def _(i):
            cols = pl.ds(pl.multiple_of(i * 256, 256), 256)
            pre = nn(rows[j, 0].reshape(512, D), w1[j, :, cols])
            cdf = 0.5 * (1.0 + lax.erf(pre * root_half))
            act[j, :, cols] = (pre * cdf).astype(BF)
            slope = cdf + pre * (density_scale * jnp.exp(-0.5 * pre * pre))
            grad = nt(rows[j, 1].reshape(512, D), w2[j, cols, :])
            hid[j, :, cols] = (grad * slope).astype(BF)

    def partial(j, h):
        @pl.loop(0, 5)
        def _(i):
            at = pl.ds(pl.multiple_of(h * HALF + i * 128, 128), 128)
            cols = pl.ds(pl.multiple_of(i * 128, 128), 128)
            pb[j, h, :, :, :, cols] = nt(hid[j], w1[j, at, :]).astype(BF).reshape(4, 4, 32, 128)

    def grads(j):
        @pl.loop(0, 5)
        def _(i):
            cols = pl.ds(pl.multiple_of(i * 256, 256), 256)
            g1[j, cols, :] = tn(rows[j, 0, :, :, :, cols].reshape(512, 256), hid[j]).astype(BF)
            g2[j, :, cols] = tn(act[j], rows[j, 1, :, :, :, cols].reshape(512, 256)).astype(BF)

    far, up, dn = (x + 2) % 4, (x + 1) % 4, (x + 3) % 4
    lo, hi = pl.ds(0, 2), pl.ds(2, 2)

    def add(*refs):
        total = refs[0][...].astype(F32)
        for ref in refs[1:]:
            total = total + ref[...].astype(F32)
        return total.astype(BF)

    def px_send(j, h):
        v = pb.at[j, h]
        return [
            go(rc(v.at[far, lo], xr1.at[j, h, 0], rx_s.at[j, h, 0], rx_r.at[j, h, 0], dev_x(1))),
            go(rc(v.at[far, hi], xr1.at[j, h, 1], rx_s.at[j, h, 1], rx_r.at[j, h, 1], dev_x(3))),
            go(rc(v.at[up, hi], xr2.at[j, h, 0, hi], rx_s.at[j, h, 2], rx_r.at[j, h, 2], dev_x(1))),
            go(rc(v.at[dn, lo], xr2.at[j, h, 1, lo], rx_s.at[j, h, 3], rx_r.at[j, h, 3], dev_x(3))),
        ]

    def px_fwd(j, h, sent):
        v = pb.at[j, h]
        sent[0].wait_recv()
        v[up, lo] = add(v.at[up, lo], xr1.at[j, h, 0])
        a = go(rc(v.at[up, lo], xr2.at[j, h, 0, lo], rx_s.at[j, h, 4], rx_r.at[j, h, 4], dev_x(1)))
        sent[1].wait_recv()
        v[dn, hi] = add(v.at[dn, hi], xr1.at[j, h, 1])
        b = go(rc(v.at[dn, hi], xr2.at[j, h, 1, hi], rx_s.at[j, h, 5], rx_r.at[j, h, 5], dev_x(3)))
        return [a, b, sent[2], sent[3]]

    def py_send(j, h, sent):
        arrive(sent)
        xs[j, h] = add(pb.at[j, h, x], xr2.at[j, h, 0], xr2.at[j, h, 1])
        return [
            go(rc(xs.at[j, h, (y + d) % 4], yr.at[j, h, d - 1], ry_s.at[j, h, d], ry_r.at[j, h, d], dev_y(d)))
            for d in (1, 3, 2)
        ]

    def p_sum(j, h, sent):
        arrive(sent)
        bb[j, h, 0] = add(xs.at[j, h, y], yr.at[j, h, 1])
        bb[j, h, 1] = add(yr.at[j, h, 0], yr.at[j, h, 2])

    def qy_send(j, h):
        return [
            go(rc(pb.at[j, h, :, (y + d) % 4], yq.at[d - 1], ry_s.at[j, h, d], ry_r.at[j, h, d], dev_y(d)))
            for d in (1, 3, 2)
        ]

    def qx_send(j, h, sent):
        arrive(sent)
        qs[0] = add(pb.at[j, h, :, y], yq.at[1])
        qs[1] = add(yq.at[0], yq.at[2])
        return [
            go(rc(qs.at[0, far], xr1.at[j, h, 0, 0], rx_s.at[j, h, 0], rx_r.at[j, h, 0], dev_x(1))),
            go(rc(qs.at[1, far], xr1.at[j, h, 1, 0], rx_s.at[j, h, 1], rx_r.at[j, h, 1], dev_x(3))),
            go(rc(qs.at[1, up], xr2.at[j, h, 0, 1], rx_s.at[j, h, 2], rx_r.at[j, h, 2], dev_x(1))),
            go(rc(qs.at[0, dn], xr2.at[j, h, 1, 0], rx_s.at[j, h, 3], rx_r.at[j, h, 3], dev_x(3))),
        ]

    def qx_fwd(j, h, sent):
        sent[0].wait_recv()
        qs[0, up] = add(qs.at[0, up], xr1.at[j, h, 0, 0])
        a = go(rc(qs.at[0, up], xr2.at[j, h, 0, 0], rx_s.at[j, h, 4], rx_r.at[j, h, 4], dev_x(1)))
        sent[1].wait_recv()
        qs[1, dn] = add(qs.at[1, dn], xr1.at[j, h, 1, 0])
        b = go(rc(qs.at[1, dn], xr2.at[j, h, 1, 1], rx_s.at[j, h, 5], rx_r.at[j, h, 5], dev_x(3)))
        return [a, b, sent[2], sent[3]]

    def q_sum(j, h, sent):
        arrive(sent)
        for o in range(2):
            bb[j, h, o] = add(qs.at[o, x], xr2.at[j, h, 0, o], xr2.at[j, h, 1, o])

    def zb_copy(j, k):
        to = (wide + k) % 16
        return rc(zbs.at[j, to], zbr.at[j, wide], zb_s.at[j, k], zb_r.at[j, k], dev_w(k))

    def zb_send(j):
        mb = one_hot(
            128, 64,
            lambda r: (((r >> 1) & 1) ^ rep) * 32 + (r >> 3) * 2 + (r & 1),
        )
        first = (lax.broadcasted_iota(jnp.int32, (128, HALF), 0) & 4) == 0
        both = [nn(mb, bb[j, h].reshape(64, HALF)) for h in range(2)]
        zbs[j] = jnp.where(first, both[0], both[1]).reshape(16, 8, HALF).astype(BF)

        @pl.loop(1, 16)
        def _(k):
            zb_copy(j, k).start()

        zbr[j, wide] = zbs[j, wide]

    def zb_done(j):
        @pl.loop(1, 16)
        def _(k):
            zb_copy(j, k).wait_recv()

    def turn():
        @pl.loop(0, 5)
        def _(i):
            row = lax.broadcasted_iota(jnp.int32, (256, D), 0) + i * 256
            col = lax.broadcasted_iota(jnp.int32, (256, D), 1)
            piece = (row * 52429) >> 18
            k = row - piece * 5
            zz, nn_, cc, lo_ = piece & 7, (piece >> 3) & 7, (piece >> 6) & 1, piece >> 7
            want = (((lo_ * 8 + zz) * 2 + cc) * 8 + nn_) * 5 + k
            pick = (col == want).astype(F32).astype(BF)
            tokt[pl.ds(pl.multiple_of(i * 256, 256), 256), :] = nt(pick, tok[...]).astype(BF)

    loads[3].wait()
    comb_raw = nt(gout[...], sout[...])
    com = combine[...]
    lcomb[...] = com * (comb_raw - jnp.sum(com * comb_raw, axis=1, keepdims=True))

    def step1(j, t):
        arrive(t["xg"])
        t["xgf"] = xg_fwd(j)
        t["yg"] += [yg_send(j, 3), yg_send(j, 1)]

    def step2(j, t):
        for d in (1, 3, 2):
            t["yi"][d].wait_recv()
            t["xi"][d] = xin_send(j, d)

    def step3(j, t):
        arrive(t["xgf"])
        t["yg"].append(yg_send(j, 2))

    def step4(j, t):
        for e in (0, 1, 3, 2):
            t["xf"].append(xin_fwd(j, e, t["xi"][e]))

    def step5(j, t):
        for e in (0, 1):
            t["xi"][e][1].wait_recv()
        for e in (2, 3):
            t["xi"][e][0].wait_recv()
        arrive(t["xf"])
        for out, own in t["yg"]:
            arrive(out)
            own.wait()

    def start_g(j):
        return dict(xg=xg_send(j), yg=[yg_send(j, 0)], xf=[])

    def start_i(j, t):
        t["yi"] = yin_send(j)
        t["xi"] = {0: xin_send(j, 0)}

    z_done(1, 0)
    z_send(1, 1)
    spread(1, 0)
    t0 = start_g(0)
    z_done(0, 0)
    z_send(0, 1)
    spread(0, 0)
    start_i(0, t0)
    turn()
    step1(0, t0)
    step2(0, t0)
    step3(0, t0)
    z_done(1, 1)
    spread(1, 1)
    z_done(0, 1)
    spread(0, 1)
    step4(0, t0)
    t1 = start_g(1)
    start_i(1, t1)
    loads[4].wait()
    loads[5].wait()
    step5(0, t0)
    hidden(0)
    step1(1, t1)
    step2(1, t1)
    partial(0, 0)
    partial(0, 1)
    step3(1, t1)
    step4(1, t1)
    p00 = px_send(0, 0)
    p01 = px_send(0, 1)
    step5(1, t1)
    hidden(1)
    partial(1, 1)
    q1 = qy_send(1, 1)
    p00 = px_fwd(0, 0, p00)
    p01 = px_fwd(0, 1, p01)
    partial(1, 0)
    p10 = px_send(1, 0)
    p00 = py_send(0, 0, p00)
    p01 = py_send(0, 1, p01)
    p10 = px_fwd(1, 0, p10)
    q1 = qx_send(1, 1, q1)
    p_sum(0, 0, p00)
    p_sum(0, 1, p01)
    zb_send(0)
    q1 = qx_fwd(1, 1, q1)
    p10 = py_send(1, 0, p10)
    q_sum(1, 1, q1)
    p_sum(1, 0, p10)
    zb_send(1)
    grads(0)
    grads(1)
    zb_done(0)
    zb_done(1)

    recv = zbr[...].astype(F32).reshape(256, HALF).astype(BF)
    halves = []
    for h in range(2):
        q = one_hot(
            128, 256,
            lambda s: ((s >> 1) & 1) * 128 + ((s >> 2) & 15) * 8 + h * 4 + (s >> 6) * 2 + (s & 1),
        )
        halves.append(nn(q, recv).astype(BF))
    slot_back = jnp.concatenate(halves, axis=1)
    disp_raw = nt(tok[...], slot_back)
    dis = dispatch[...]
    ldisp = dis * (disp_raw - jnp.sum(dis * disp_raw, axis=0, keepdims=True))
    lg = (lcomb[...] + ldisp).astype(BF)
    rt[...] = nn(tokt[...], lg).reshape(32, 40, 128).astype(BF)

    def plane_copy(k):
        cc, xx, yy = (c + k) % 2, (x + k // 2) % 4, (y + k // 8) % 4
        block = (yy % 2) * 16 + cc * 8 + (yy // 2) * 4 + xx
        dev = (yy % 2, z * 2 + cc, (yy // 2) * 4 + xx)
        return rc(rt.at[block], rr.at[k], pl_s.at[k], pl_r.at[k], dev)

    @pl.loop(1, 32)
    def _(k):
        plane_copy(k).start()

    rr[0] = rt[rep * 16 + c * 8 + nar]
    gx[0] = (nt(lg, routing[...]) + nn(dis.astype(BF), slot_back)).astype(BF)

    @pl.loop(1, 32)
    def _(k):
        plane_copy(k).wait_recv()

    total = jnp.sum(rr[...].astype(F32), axis=0)
    for i in range(8):
        ex[i, 0:5] = total[5 * i:5 * i + 5]

    def s4_copy(k):
        return rc(ex.at[(z + k) % 8], rr4.at[k], s4_s.at[k], s4_r.at[k], dev_w(2 * k))

    @pl.loop(1, 8)
    def _(k):
        s4_copy(k).start()

    rr4[0] = ex[z]

    @pl.loop(1, 8)
    def _(k):
        s4_copy(k).wait_recv()

    tot = rr4[0]
    for i in range(1, 8):
        tot = tot + rr4[i]
    gr_ref[...] = tot[0:5]

    @pl.loop(1, 8)
    def _(k):
        s4_copy(k).wait_send()

    @pl.loop(1, 16)
    def _(k):
        for j in range(2):
            z_copy(0, j, k).wait_send()
            z_copy(1, j, k).wait_send()
            zb_copy(j, k).wait_send()

    @pl.loop(1, 32)
    def _(k):
        plane_copy(k).wait_send()

    for copy in pending:
        copy.wait_send()


def local(tokens, routing, grad_out, slot_out, w_first, w_second):
    in_hbm = pl.BlockSpec(memory_space=pltpu.HBM)
    in_vmem = pl.BlockSpec(memory_space=pltpu.VMEM)
    v = pltpu.VMEM
    dma = pltpu.SemaphoreType.DMA
    shapes = (
        ((1, 256, D), BF),
        ((5, 128), F32),
        ((2, D, 512), BF),
        ((2, 512, D), BF),
    )
    return pl.pallas_call(
        kernel,
        out_shape=tuple(OUT(*shape) for shape in shapes),
        in_specs=[in_hbm] * 6,
        out_specs=(in_vmem,) * 4,
        scratch_shapes=[
            v((256, D), BF), v((D, 128), BF), v((256, D), BF), v((128, D), BF),
            v((2, D, 512), BF), v((2, 512, D), BF),
            v((256, 128), F32), v((256, 128), F32), v((256, 128), F32),
            v((2, 2, 16, 8, HALF), BF), v((2, 2, 16, 8, HALF), BF),
            v((2, 2, 32, D), BF), v((2, 4, 2, 32, D), BF), v((2, 2, 4, 4, 32, D), BF),
            v((2, 512, 512), BF), v((2, 512, 512), BF), v((2, 2, 4, 4, 32, HALF), BF),
            v((2, 2, 2, 2, 32, HALF), BF), v((2, 2, 2, 4, 32, HALF), BF), v((2, 2, 4, 32, HALF), BF),
            v((2, 2, 3, 32, HALF), BF), v((3, 4, 32, HALF), BF), v((2, 4, 32, HALF), BF),
            v((2, 2, 2, 32, HALF), BF),
            v((2, 16, 8, HALF), BF), v((2, 16, 8, HALF), BF),
            v((D, 256), BF), v((32, 40, 128), BF), v((32, 40, 128), BF),
            v((8, 8, 128), F32), v((8, 8, 128), F32),
            dma((6,)), dma((2, 4)),
            dma((2, 2, 16)), dma((2, 2, 16)), dma((2, 4)), dma((2, 4)), dma((2, 4, 3)), dma((2, 4, 3)),
            dma((2, 4)), dma((2, 4)), dma((2, 4, 4)), dma((2, 4, 4)),
            dma((2, 2, 6)), dma((2, 2, 6)), dma((2, 2, 4)), dma((2, 2, 4)), dma((2, 16)), dma((2, 16)),
            dma((32,)), dma((32,)), dma((8,)), dma((8,)),
        ],
        compiler_params=pltpu.CompilerParams(
            collective_id=0, has_side_effects=True, vmem_limit_bytes=LIMIT * 2**20
        ),
    )(tokens, routing, grad_out, slot_out, w_first, w_second)

def solution(mesh):
    return jax.shard_map(
        local,
        mesh=mesh,
        in_specs=(
            P(("rep", "wide", "narrow"), None, None),
            P(),
            P(("rep", "wide", "narrow"), None, None),
            P(("rep", "wide", "narrow"), None, None),
            P(("rep", "wide"), None, "narrow"),
            P(("rep", "wide"), "narrow", None),
        ),
        out_specs=(
            P(("rep", "wide", "narrow"), None, None),
            P(("rep", "wide", "narrow"), None),
            P(("rep", "wide"), None, "narrow"),
            P(("rep", "wide"), "narrow", None),
        ),
        check_vma=False,
    )
```
